256 devices in a mesh: box: 64 (over y, z, core), chan: 4 (over x).
Axes of the slice: x: 4, y: 4, z: 8, core: 2. Of those that a mesh axis runs over, the one named last changes fastest.
Arguments:
- features: bfloat16 [64, 524288], P('chan', 'box'), may hold values from -6 to 6
- harmonics: bfloat16 [49, 524288], P(None, 'box'), may hold values from -0.75 to 0.75
- atom_leaf: int32 [524288], P('box'), may hold values from 0 to 127
- leaf_sources: int32 [8192, 189], P('box'), may hold values from -1 to 8191, as said below
- coarse_sources: int32 [128, 64], P('box'), may hold values from 0 to 127, as said below
- coarse_class: int32 [128, 64], P('box'), may hold values from 0 to 315
- child_to_parent: bfloat16 [8, 49, 49], replicated, may hold values from -0.3125 to 0.3125
- parent_to_child: bfloat16 [8, 49, 49], replicated, may hold values from -0.875 to 0.875
- leaf_transfer: bfloat16 [189, 49, 49], replicated, may hold values from -0.0625 to 0.0625
- coarse_transfer: bfloat16 [316, 49, 49], replicated, may hold values from -0.109375 to 0.109375
- mix_weight: bfloat16 [7, 64, 64], replicated, may hold values from -0.75 to 0.75
Outputs:
- field: bfloat16 [64, 524288], P('chan', 'box')
The draws below stay inside these ranges and needn't reach their ends.
Inputs may be any that keep to these rules, and one draw needn't show every extreme that they name: `leaf_sources`: -1 marks an empty slot; every other entry is a leaf box other than the target itself, of the target's device's 128 leaves or of the 128 leaves just before or just after them; the outermost leaves of both neighbouring ranges occur wherever they exist. `coarse_sources`: the 64 sources of a coarse box are distinct coarse boxes other than itself.
All inputs are finite; a program needn't handle non-finite values.
Results may differ from the reference program's by a relative error of at most 0.015.
Values may be sent and summed in bfloat16 or wider, within the bound.
A program may use at most 64 MiB of HBM per device.

```python
import jax
import jax.numpy as jnp
from jax import lax

DEG = 7
K = 49
CH = 64
S = 189
OC = 316
LB = 128
ATOM_DEV = 8192
NLEAF = 8192
NCB = 128
SC = 64
ATOMS = 524288
N_BOX = 64


def draw_leaf_sources(key, part):
    key = jax.random.fold_in(key, 11)
    pick_key, empty_key = jax.random.split(key)
    target = jnp.arange(NLEAF, dtype=jnp.int32)[:, None]
    first_leaf = target // LB * LB - LB
    offsets = jax.random.randint(pick_key, (NLEAF, S), 0, 3 * LB, dtype=jnp.int32)
    source = first_leaf + offsets
    empty = jax.random.randint(empty_key, (NLEAF, S), 0, 4, dtype=jnp.int32) == 0
    slot = jnp.arange(S, dtype=jnp.int32)[None, :]
    local = target % LB
    low_edge = (local == 0) & (slot == 0)
    high_edge = (local == LB - 1) & (slot == 1)
    source = jnp.where(empty | (source == target), -1, source)
    source = jnp.where(low_edge, first_leaf, source)
    source = jnp.where(high_edge, first_leaf + 3 * LB - 1, source)
    source = jnp.where((source < 0) | (source >= NLEAF), -1, source)
    return source.astype(jnp.int32)


def draw_coarse_sources(key, part):
    key = jax.random.fold_in(key, 12)
    scores = jax.random.randint(key, (NCB, NCB - 1), 0, 1 << 20, dtype=jnp.int32)
    distinct = scores * NCB + jnp.arange(NCB - 1, dtype=jnp.int32)[None, :]
    ranked = jnp.argsort(distinct, axis=1)[:, :SC].astype(jnp.int32)
    target = jnp.arange(NCB, dtype=jnp.int32)[:, None]
    return ((target + 1 + ranked) % NCB).astype(jnp.int32)


def place_ends(array, stream_key, smallest, top_value):
    shape = array.shape
    spot = [jax.random.randint(jax.random.fold_in(stream_key, axis), (), 0, shape[axis]) for axis in range(len(shape))]
    array = array.at[tuple(spot)].set(smallest)
    longest = shape.index(max(shape))
    spot[longest] = (spot[longest] + 1) % shape[longest]
    return array.at[tuple(spot)].set(top_value)


def shard_levels(rng, dims, cuts, smallest, high):
    loudness = 1.0
    for dim, parts in cuts:
        steps = jax.random.uniform(jax.random.fold_in(jax.random.fold_in(rng, 6), dim), (parts,), jnp.float32, smallest / len(cuts), high / len(cuts))
        loudness = loudness * jnp.repeat(jnp.exp(steps), dims[dim] // parts).reshape((-1,) + (1,) * (len(dims) - 1 - dim))
    return loudness


def gaussian(rng, dims, width, bound, cuts=(), kind=jnp.bfloat16):
    values = width * jax.random.normal(rng, dims, jnp.float32)
    if cuts:
        values = values * shard_levels(rng, dims, cuts, -0.22, 0.18)
    return jnp.clip(values, -bound, bound).astype(kind)


def setup_inputs(seed: int = 0) -> dict:
    key_list = jax.random.split(jax.random.key(seed), 12)
    return {
        "features": gaussian(key_list[0], (CH, ATOMS), 1.0, 6.0, ((0, 4), (1, 64))),
        "harmonics": gaussian(key_list[1], (K, ATOMS), 0.125, 0.75, ((1, 64),)),
        "atom_leaf": place_ends(jax.random.randint(key_list[2], (ATOMS,), 0, LB), jax.random.fold_in(key_list[2], 1), 0, LB - 1).astype(jnp.int32),
        "leaf_sources": draw_leaf_sources(jax.random.fold_in(key_list[11], 71), 0),
        "coarse_sources": draw_coarse_sources(jax.random.fold_in(key_list[11], 71), 0),
        "coarse_class": place_ends(jax.random.randint(key_list[5], (NCB, SC), 0, OC), jax.random.fold_in(key_list[5], 1), 0, OC - 1).astype(jnp.int32),
        "child_to_parent": gaussian(key_list[6], (8, K, K), (8 * K) ** -0.5, 0.3125),
        "parent_to_child": gaussian(key_list[7], (8, K, K), K ** -0.5, 0.875),
        "leaf_transfer": gaussian(key_list[8], (S, K, K), (K * S) ** -0.5, 0.0625),
        "coarse_transfer": gaussian(key_list[9], (OC, K, K), (K * SC) ** -0.5, 0.109375),
        "mix_weight": gaussian(key_list[10], (DEG, CH, CH), CH ** -0.5, 0.75),
    }


def upward(children, table):
    coeffs, chans, count = children.shape
    grouped = children.astype(jnp.float32).reshape(coeffs, chans, count // 8, 8)
    result = jnp.einsum("oqk,kcmo->qcm", table.astype(jnp.float32), grouped)
    return result.astype(jnp.bfloat16)


def downward(parents, table):
    coeffs, chans, count = parents.shape
    spread = jnp.einsum("oqk,kcp->qcpo", table.astype(jnp.float32), parents.astype(jnp.float32))
    return spread.reshape(coeffs, chans, count * 8)


def mix_degrees(leaf_local, mix_weight):
    pieces = []
    for degree in range(DEG):
        row_block = leaf_local[degree * degree:(degree + 1) * (degree + 1)].astype(jnp.float32)
        pieces.append(jnp.einsum("xc,kcb->kxb", mix_weight[degree].astype(jnp.float32), row_block))
    return jnp.concatenate(pieces, 0).astype(jnp.bfloat16)


def reference(features, harmonics, atom_leaf, leaf_sources, coarse_sources, coarse_class,
              child_to_parent, parent_to_child, leaf_transfer, coarse_transfer, mix_weight):
    feat_blocks = features.reshape(CH, N_BOX, ATOM_DEV).transpose(1, 0, 2)
    harm_blocks = harmonics.reshape(K, N_BOX, ATOM_DEV).transpose(1, 0, 2)
    leaf_blocks = atom_leaf.reshape(N_BOX, ATOM_DEV)

    def moments(inputs):
        feat_block, harm_block, leaf_block = inputs
        products = (harm_block.astype(jnp.float32)[:, None, :] * feat_block.astype(jnp.float32)[None]).astype(jnp.bfloat16)
        summed = jax.ops.segment_sum(jnp.moveaxis(products.astype(jnp.float32), 2, 0), leaf_block, num_segments=LB)
        return jnp.moveaxis(summed, 0, 2).astype(jnp.bfloat16)

    per_device = lax.map(moments, (feat_blocks, harm_blocks, leaf_blocks))
    leaf_multi = per_device.transpose(1, 2, 0, 3).reshape(K, CH, NLEAF)

    padded = jnp.concatenate([leaf_multi, jnp.zeros((K, CH, 1), jnp.bfloat16)], 2)
    columns = jnp.where(leaf_sources >= 0, leaf_sources, NLEAF).astype(jnp.int32)

    def slot_step(running, inputs):
        column, matrix = inputs
        picked = jnp.take(padded, column, axis=2).astype(jnp.float32)
        return running + jnp.einsum("qk,kcb->qcb", matrix.astype(jnp.float32), picked), None

    far_leaf, _ = lax.scan(slot_step, jnp.zeros((K, CH, NLEAF), jnp.float32), (columns.T, leaf_transfer))

    mid_multi = upward(leaf_multi, child_to_parent)
    coarse_multi = upward(mid_multi, child_to_parent)
    picked = jnp.take(coarse_multi, coarse_sources.reshape(-1), axis=2).reshape(K, CH, NCB, SC).astype(jnp.float32)
    matrices = jnp.take(coarse_transfer, coarse_class.reshape(-1), axis=0).reshape(NCB, SC, K, K).astype(jnp.float32)
    coarse_local = jnp.einsum("tjqk,kctj->qct", matrices, picked).astype(jnp.bfloat16)

    mid_local = downward(coarse_local, parent_to_child).astype(jnp.bfloat16)
    leaf_local = (downward(mid_local, parent_to_child) + far_leaf).astype(jnp.bfloat16)
    mixed = mix_degrees(leaf_local, mix_weight)
    mixed_blocks = mixed.reshape(K, CH, N_BOX, LB).transpose(2, 0, 1, 3)

    def evaluate(inputs):
        local_block, harm_block, leaf_block = inputs
        selected = jnp.take(local_block, leaf_block, axis=2).astype(jnp.float32)
        return jnp.einsum("ka,kca->ca", harm_block.astype(jnp.float32), selected).astype(jnp.bfloat16)

    outputs = lax.map(evaluate, (mixed_blocks, harm_blocks, leaf_blocks))
    return outputs.transpose(1, 0, 2).reshape(CH, ATOMS)
```

```python
import jax
import jax.numpy as jnp
import numpy as np
from jax import lax
from jax.experimental import pallas as pl
from jax.experimental.pallas import tpu as pltpu
from jax.sharding import PartitionSpec as P

F32 = jnp.float32
BF16 = jnp.bfloat16
K = 49
KP = 64
CH = 16
CP = 8
LB = 128
ATOMS = 8192
SLOTS = 189
NT = (((1,), (1,)), ((), ()))
VMEM = pl.BlockSpec(memory_space=pltpu.VMEM)
SMEM = pl.BlockSpec(memory_space=pltpu.SMEM)
DEGREE = np.array([int(np.sqrt(k)) for k in range(K)])


def dot_nt(a, b):
    return lax.dot_general(a, b, NT, preferred_element_type=F32)


def twice(block):
    wide = jnp.concatenate([block.astype(F32), jnp.zeros((K, 128 - K), F32)], 1)
    tall = jnp.concatenate([wide, jnp.zeros((KP - K, 128), F32)], 0)
    return jnp.concatenate([tall, pltpu.roll(tall, KP, 1)], 0).astype(BF16)


def moments_kernel(feat, harm, leaf, up, tiles_out, coarse_out, hpad, acc, rows32, mid32):
    step = 512
    hpad[...] = jnp.concatenate([harm[...].astype(F32), jnp.zeros((KP - K, ATOMS), F32)], 0).astype(BF16)
    acc[...] = jnp.zeros_like(acc)

    def turn(i, carry):
        at = pl.ds(pl.multiple_of(i * step, step), step)
        onehot = jnp.where(
            leaf[:, at] == lax.broadcasted_iota(jnp.int32, (LB, step), 0), 1.0, 0.0
        ).astype(BF16)
        h = hpad[:, at]
        f = feat[:, at]
        for group in range(4):
            products = jnp.concatenate([h * f[4 * group + c : 4 * group + c + 1] for c in range(4)], 0)
            cols = slice(group * 256, group * 256 + 256)
            acc[:, cols] += dot_nt(onehot, products)
        return carry

    lax.fori_loop(0, ATOMS // step, turn, 0)
    for pair in range(CP):
        part = acc[:, pair * 128 : pair * 128 + 128].astype(BF16).astype(F32)
        rows32[pl.ds(pair, LB, stride=CP), :] = part
    tiles = rows32[...].astype(BF16)
    tiles_out[...] = tiles
    tables = [twice(up[o]) for o in range(8)]
    by_child = rows32[...].reshape(16, 8, CP, 128)
    mid = jnp.zeros((128, 128), F32)
    for o in range(8):
        mid += dot_nt(by_child[:, o].reshape(128, 128).astype(BF16), tables[o])
    mid32[...] = mid.astype(BF16).astype(F32)
    mids = mid32[...].reshape(2, 8, CP, 128)
    coarse = jnp.zeros((16, 128), F32)
    for o in range(8):
        coarse += dot_nt(mids[:, o].reshape(16, 128).astype(BF16), tables[o])
    coarse_out[...] = coarse.astype(BF16)


def far_kernel(
    index, csource, cclass, before, own, after, coarse, transfer, ctransfer, down,
    out, table, weights, call32, far32, local32, mid32,
):
    for place, block in enumerate((before, own, after)):
        table[place * 1024 : place * 1024 + 1024, :] = block[...].astype(F32)
    table[3072:3080, :] = jnp.zeros((8, 128), F32)
    call32[...] = coarse[...].astype(F32)

    def build(i, carry):
        for r in range(9):
            j = i * 9 + r
            weights[j] = twice(transfer[j])
        return carry

    lax.fori_loop(0, 21, build, 0)
    for j in range(SLOTS, 192):
        weights[j] = jnp.zeros((128, 128), BF16)

    def block(tb, carry):
        def chunk(jc, acc):
            def pick(jj, t):
                row = index[tb * 6 + jc, jj % 8, (jj // 8) * 32 + t]
                return table[pl.ds(pl.multiple_of(row, 8), 8), :]

            parts = []
            for jj in range(32):
                pairs = [
                    jnp.concatenate([pick(jj, t), pick(jj, t + 1)], 0).astype(BF16) for t in range(0, 32, 2)
                ]
                parts.append(jnp.concatenate(pairs, 0))
            lhs = jnp.concatenate(parts, 1)
            rhs = jnp.concatenate([weights[jc * 32 + jj] for jj in range(32)], 1)
            return acc + dot_nt(lhs, rhs)

        total = lax.fori_loop(0, 6, chunk, jnp.zeros((256, 128), F32))
        far32[pl.ds(pl.multiple_of(tb * 256, 256), 256), :] = total
        return carry

    lax.fori_loop(0, 4, block, 0)

    def coarse_target(target):
        def slots(i, acc):
            for r in range(8):
                j = target * 64 + i * 8 + r
                x = call32[pl.ds(pl.multiple_of(csource[j] * 8, 8), 8), :]
                both = jnp.concatenate([x, pltpu.roll(x, KP, 1)], 0)[:, :K].astype(BF16)
                acc = acc + dot_nt(both, ctransfer[cclass[j]])
            return acc

        acc = lax.fori_loop(0, 8, slots, jnp.zeros((16, K), F32))
        wide = jnp.concatenate([acc, jnp.zeros((16, 128 - K), F32)], 1)
        return wide[:8] + pltpu.roll(wide[8:], KP, 1)

    coarse_local = jnp.concatenate([coarse_target(0), coarse_target(1)], 0).astype(BF16)
    tables = [twice(down[o]) for o in range(8)]
    for o in range(8):
        mid = dot_nt(coarse_local, tables[o])
        mid32[o * 8 : o * 8 + 8, :] = mid[:8]
        mid32[64 + o * 8 : 64 + o * 8 + 8, :] = mid[8:]
    mids = mid32[...].astype(BF16)
    for o in range(8):
        local32[:, o] = dot_nt(mids, tables[o]).reshape(16, CP, 128)
    far32[...] += local32[...].reshape(1024, 128)
    for pair in range(CP):
        out[:, pair * 128 : pair * 128 + 128] = far32[pl.ds(pair, LB, stride=CP), :].astype(BF16)


def field_kernel(harm, leaf, local, wide_mix, out, acc, mixed):
    acc[...] = jnp.zeros_like(acc)
    for dev in range(4):
        def mix(i, carry):
            cols = pl.ds(pl.multiple_of(i * 512, 512), 512)
            weight = wide_mix[:, pl.ds(pl.multiple_of(dev * 1024 + i * 512, 512), 512)].astype(F32)
            lane = lax.rem(lax.broadcasted_iota(jnp.int32, (16, 512), 1), KP)
            lhs = jnp.concatenate([jnp.where(lane == q, weight, 0.0).astype(BF16) for q in range(K)], 0)
            acc[...] += dot_nt(lhs, local[dev, :, cols])
            return carry

        lax.fori_loop(0, 2, mix, 0)
    mixed[...] = acc[...].astype(BF16)
    step = 256

    def turn(i, carry):
        at = pl.ds(pl.multiple_of(i * step, step), step)
        onehot = jnp.where(
            leaf[:, at] == lax.broadcasted_iota(jnp.int32, (LB, step), 0), 1.0, 0.0
        ).astype(BF16)
        picked = jnp.dot(mixed[...], onehot, preferred_element_type=F32)
        h = harm[:, at].astype(F32)
        total = jnp.zeros((CH, step), F32)
        for q in range(K):
            total += h[q : q + 1] * picked[q * 16 : q * 16 + 16]
        out[:, at] = total.astype(BF16)
        return carry

    lax.fori_loop(0, ATOMS // step, turn, 0)


def on_device(
    features, harmonics, atom_leaf, leaf_sources, coarse_sources, coarse_class,
    child_to_parent, parent_to_child, leaf_transfer, coarse_transfer, mix_weight,
):
    params = pltpu.CompilerParams(vmem_limit_bytes=60 << 20)
    leaf_row = atom_leaf.reshape(1, ATOMS)
    tiles, coarse = pl.pallas_call(
        moments_kernel,
        out_shape=(jax.ShapeDtypeStruct((1024, 128), BF16), jax.ShapeDtypeStruct((16, 128), BF16)),
        in_specs=[VMEM] * 4,
        out_specs=(VMEM, VMEM),
        scratch_shapes=[
            pltpu.VMEM((KP, ATOMS), BF16),
            pltpu.VMEM((LB, 1024), F32),
            pltpu.VMEM((1024, 128), F32),
            pltpu.VMEM((128, 128), F32),
        ],
        compiler_params=params,
        name="moments",
    )(features, harmonics, leaf_row, child_to_parent)

    peers = lax.axis_size("box")
    up = [(i, i + 1) for i in range(peers - 1)]
    down = [(i + 1, i) for i in range(peers - 1)]
    before = lax.ppermute(tiles, "box", up)
    after = lax.ppermute(tiles, "box", down)
    coarse_all = lax.all_gather(coarse, "box", axis=0, tiled=True)

    first = lax.axis_index("box") * LB - LB
    index = jnp.where(leaf_sources >= 0, (leaf_sources - first) * 8, 3072)
    index = jnp.pad(index, ((0, 0), (0, 3)), constant_values=3072)
    index = index.reshape(4, 32, 6, 4, 8).transpose(0, 2, 4, 3, 1).reshape(24, 8, 128)

    local = pl.pallas_call(
        far_kernel,
        out_shape=jax.ShapeDtypeStruct((LB, 1024), BF16),
        in_specs=[SMEM] * 3 + [VMEM] * 7,
        out_specs=VMEM,
        scratch_shapes=[
            pltpu.VMEM((3080, 128), F32),
            pltpu.VMEM((192, 128, 128), BF16),
            pltpu.VMEM((1024, 128), F32),
            pltpu.VMEM((1024, 128), F32),
            pltpu.VMEM((16, 8, CP, 128), F32),
            pltpu.VMEM((128, 128), F32),
        ],
        compiler_params=params,
        name="far",
    )(
        index, coarse_sources.reshape(-1), coarse_class.reshape(-1), before, tiles, after,
        coarse_all, leaf_transfer, coarse_transfer, parent_to_child,
    )
    local_all = lax.all_gather(local, "chan", axis=0)

    start = lax.axis_index("chan") * CH
    mine = lax.dynamic_slice_in_dim(mix_weight, start, CH, 1)
    wide = jnp.pad(mine[DEGREE], ((0, KP - K), (0, 0), (0, 0)))
    wide = wide.transpose(1, 2, 0).reshape(CH, 64 * KP)
    return pl.pallas_call(
        field_kernel,
        out_shape=jax.ShapeDtypeStruct((CH, ATOMS), BF16),
        in_specs=[VMEM] * 4,
        out_specs=VMEM,
        scratch_shapes=[pltpu.VMEM((K * 16, 128), F32), pltpu.VMEM((K * 16, 128), BF16)],
        compiler_params=params,
        name="field",
    )(harmonics, leaf_row, local_all, wide)


def solution(mesh):
    placed = (
        P("chan", "box"), P(None, "box"), P("box"), P("box", None), P("box", None), P("box", None),
        P(), P(), P(), P(), P(),
    )
    return jax.shard_map(
        on_device, mesh=mesh, in_specs=placed, out_specs=P("chan", "box"), check_vma=False
    )
```

```python
import jax
import jax.numpy as jnp
import numpy as np
from jax import lax
from jax.experimental import pallas as pl
from jax.experimental.pallas import tpu as pltpu
from jax.sharding import PartitionSpec as P

F32 = jnp.float32
BF16 = jnp.bfloat16
I32 = jnp.int32
MESH = pl.DeviceIdType.MESH
K = 49
KP = 64
CH = 16
CP = 8
LB = 128
ATOMS = 8192
SLOTS = 189
CLASSES = 316
BOXES = 64
CHANS = 4
EMPTY = 3 * LB * CP
NT = (((1,), (1,)), ((), ()))
VMEM = pl.BlockSpec(memory_space=pltpu.VMEM)
ANY = pl.BlockSpec(memory_space=pl.ANY)
DEGREE = np.array([int(np.sqrt(k)) for k in range(K)])


def dot_nt(a, b):
    return lax.dot_general(a, b, NT, preferred_element_type=F32)


def below(block, rows):
    return jnp.concatenate([block, jnp.zeros((rows - block.shape[0], block.shape[1]), block.dtype)], 0)


def octant_tables(ref, wide):
    wide[...] = jnp.zeros_like(wide)
    wide[0 : K * 8, 0:K] = ref[...].astype(F32).reshape(K * 8, K)
    tables = []
    for o in range(8):
        part = wide[pl.ds(o, KP, stride=8), :]
        tables.append(jnp.concatenate([part, pltpu.roll(part, KP, 1)], 0).astype(BF16))
    return tables


def onehot_rows(row, count):
    shape = (count, row.shape[1])
    return jnp.where(row == lax.broadcasted_iota(I32, shape, 0), 1.0, 0.0).astype(BF16)


def far_kernel(
    feat, harm, leaf, sources, csource, cclass, up, down, transfer, ctransfer,
    out,
    hpad, acc, own32, own, before, after, mid32, wide, call, transfer_v, ctransfer_v, byrow, weights,
    index_v, index_s, table, far32, local32, picked32, source32,
    load_sem, index_sem, halo_send, halo_recv, call_send, call_recv, chan_send, chan_recv,
):
    box = lax.axis_index("box")
    chan = lax.axis_index("chan")
    load_a = pltpu.make_async_copy(transfer, transfer_v, load_sem.at[0])
    load_b = pltpu.make_async_copy(ctransfer, ctransfer_v, load_sem.at[1])
    load_a.start()
    load_b.start()
    barrier = pltpu.get_barrier_semaphore()

    def greet(d, carry):
        pl.semaphore_signal(
            barrier, inc=1, device_id={"box": lax.rem(box + d, BOXES)}, device_id_type=MESH
        )
        return carry

    lax.fori_loop(1, BOXES, greet, 0)
    for d in range(1, CHANS):
        pl.semaphore_signal(
            barrier, inc=1, device_id={"chan": lax.rem(chan + d, CHANS)}, device_id_type=MESH
        )

    step = 512
    hpad[...] = below(harm[...].astype(F32), KP).astype(BF16)
    acc[...] = jnp.zeros_like(acc)

    def turn(i, carry):
        at = pl.ds(pl.multiple_of(i * step, step), step)
        onehot = onehot_rows(leaf[:, at], LB)
        h = hpad[:, at]
        f = feat[:, at]
        for group in range(4):
            products = jnp.concatenate([h * f[4 * group + c : 4 * group + c + 1] for c in range(4)], 0)
            cols = slice(group * 256, group * 256 + 256)
            acc[:, cols] += dot_nt(onehot, products)
        return carry

    lax.fori_loop(0, ATOMS // step, turn, 0)
    for pair in range(CP):
        part = acc[:, pair * 128 : pair * 128 + 128].astype(BF16).astype(F32)
        own32[pl.ds(pair, LB, stride=CP), :] = part
    own[...] = own32[...].astype(BF16)

    pl.semaphore_wait(barrier, BOXES - 1 + CHANS - 1)
    right = {"box": lax.rem(box + 1, BOXES)}
    left = {"box": lax.rem(box + BOXES - 1, BOXES)}
    halos = [
        pltpu.make_async_remote_copy(
            src_ref=own, dst_ref=slot, send_sem=halo_send.at[i], recv_sem=halo_recv.at[i],
            device_id=where, device_id_type=MESH,
        )
        for i, (slot, where) in enumerate(((before, right), (after, left)))
    ]
    for copy in halos:
        copy.start()

    tables = octant_tables(up, wide)
    children = own32[...].reshape(16, 8, CP, 128)
    mid = jnp.zeros((128, 128), F32)
    for o in range(8):
        mid += dot_nt(children[:, o].reshape(128, 128).astype(BF16), tables[o])
    mid32[...] = mid.astype(BF16).astype(F32)
    mids = mid32[...].reshape(2, 8, CP, 128)
    coarse = jnp.zeros((16, 128), F32)
    for o in range(8):
        coarse += dot_nt(mids[:, o].reshape(16, 128).astype(BF16), tables[o])
    mine = call.at[pl.ds(pl.multiple_of(box * 16, 16), 16)]
    mine[...] = coarse.astype(BF16)

    def call_copy(d, sender):
        rows = call.at[pl.ds(pl.multiple_of(sender * 16, 16), 16)]
        return pltpu.make_async_remote_copy(
            src_ref=rows, dst_ref=rows, send_sem=call_send.at[d], recv_sem=call_recv.at[sender],
            device_id={"box": lax.rem(box + d, BOXES)}, device_id_type=MESH,
        )

    def call_start(d, carry):
        call_copy(d, box).start()
        return carry

    lax.fori_loop(1, BOXES, call_start, 0)

    rows = jnp.clip((sources[...] - (box * LB - LB)) * CP, 0, EMPTY - CP)
    rows = jnp.where(sources[...] >= 0, rows, EMPTY)
    index_rows = jnp.concatenate([rows, jnp.full((192 - SLOTS, LB), EMPTY, I32)], 0)
    quarter = lax.broadcasted_iota(I32, (8, 128), 1) // 32
    for tb in range(4):
        for jc in range(6):
            total = jnp.zeros((8, 128), I32)
            for jq in range(4):
                g = jc * 32 + jq * 8
                part = pltpu.roll(index_rows[g : g + 8], (jq - tb) % 4 * 32, 1)
                total = jnp.where(quarter == jq, part, total)
            index_v[tb * 6 + jc] = total
    index_copy = pltpu.make_async_copy(index_v, index_s, index_sem)
    index_copy.start()

    load_a.wait()
    for half in range(2):
        byrow[(half * KP + K) * 192 : (half + 1) * KP * 192, :] = jnp.zeros(((KP - K) * 192, 128), F32)
    eye = jnp.where(
        lax.broadcasted_iota(I32, (192, SLOTS), 0) == lax.broadcasted_iota(I32, (192, SLOTS), 1), 1.0, 0.0
    ).astype(BF16)

    def turn_slots(q, carry):
        block = below(transfer_v[q].astype(F32), KP).astype(BF16)
        gap = jnp.zeros((128, SLOTS), BF16)
        both = dot_nt(eye, jnp.concatenate([block, gap, block], 0))
        byrow[pl.ds(pl.multiple_of(q * 192, 192), 192), :] = both[:, :128]
        byrow[pl.ds(pl.multiple_of((KP + q) * 192, 192), 192), :] = both[:, 128:]
        return carry

    lax.fori_loop(0, K, turn_slots, 0)

    def pack_slots(i, carry):
        for r in range(4):
            j = i * 4 + r
            weights[j] = byrow[pl.ds(j, 128, stride=192), :].astype(BF16)
        return carry

    lax.fori_loop(0, 48, pack_slots, 0)

    load_b.wait()
    class_row = jnp.concatenate([cclass[0:1, :], cclass[1:2, :]], 1)
    class_hot = onehot_rows(class_row, CLASSES)

    def pick_classes(i, carry):
        blocks = [below(ctransfer_v[i * 7 + r].astype(F32), 56).astype(BF16) for r in range(7)]
        picked32[pl.ds(pl.multiple_of(i * 392, 8), 392), :] = jnp.dot(
            jnp.concatenate(blocks, 0), class_hot, preferred_element_type=F32
        )
        return carry

    lax.fori_loop(0, 7, pick_classes, 0)
    index_copy.wait()

    table[1024:2048, :] = own32[...]
    table[3072:3080, :] = jnp.zeros((8, 128), F32)
    for copy in halos:
        copy.wait()
    table[0:1024, :] = before[...].astype(F32)
    table[2048:3072, :] = after[...].astype(F32)

    def block(tb, carry):
        def chunk(jc, acc):
            def pick(jj, t):
                row = index_s[tb * 6 + jc, jj % 8, (jj // 8) * 32 + t]
                return table[pl.ds(row, 8), :]

            parts = []
            for jj in range(32):
                pairs = [
                    jnp.concatenate([pick(jj, t), pick(jj, t + 1)], 0).astype(BF16) for t in range(0, 32, 2)
                ]
                parts.append(jnp.concatenate(pairs, 0))
            lhs = jnp.concatenate(parts, 1)
            rhs = jnp.concatenate([weights[jc * 32 + jj] for jj in range(32)], 1)
            return acc + dot_nt(lhs, rhs)

        total = lax.fori_loop(0, 6, chunk, jnp.zeros((256, 128), F32))
        far32[pl.ds(pl.multiple_of(tb * 256, 256), 256), :] = total
        return carry

    def chan_copy(tb, d, sender):
        part = out.at[sender, pl.ds(pl.multiple_of(tb * 32, 32), 32)]
        return pltpu.make_async_remote_copy(
            src_ref=part, dst_ref=part, send_sem=chan_send.at[tb, d], recv_sem=chan_recv.at[tb, sender],
            device_id={"chan": lax.rem(chan + d, CHANS)}, device_id_type=MESH,
        )

    def finish(tb, carry):
        rows = pl.ds(pl.multiple_of(tb * 256, 256), 256)
        far32[rows, :] += local32[rows, :]
        for pair in range(CP):
            part = far32[pl.ds(tb * 256 + pair, 32, stride=CP), :]
            out[chan, pl.ds(pl.multiple_of(tb * 32, 32), 32), pair * 128 : pair * 128 + 128] = part.astype(BF16)
        for d in range(1, CHANS):
            chan_copy(tb, d, chan).start()
        return carry

    lax.fori_loop(0, 2, block, 0)

    def call_wait(d, carry):
        call_copy(d, box).wait_send()
        call_copy(d, lax.rem(box + BOXES - d, BOXES)).wait_recv()
        return carry

    lax.fori_loop(1, BOXES, call_wait, 0)
    source_row = jnp.concatenate([csource[0:1, :], csource[1:2, :]], 1)
    source_hot = onehot_rows(source_row, 128)
    own32[...] = call[...].astype(F32)
    for pair in range(CP):
        flat = own32[pl.ds(pair, 128, stride=CP), :].T.astype(BF16)
        source32[pair * 128 : pair * 128 + 128, :] = jnp.dot(flat, source_hot, preferred_element_type=F32)
    first_half = lax.broadcasted_iota(I32, (16, 128), 1) < KP

    def contract(i, acc):
        lhs, rhs = [], []
        for r in range(7):
            k = i * 7 + r
            rhs.append(picked32[pl.ds(k, K, stride=56), :].astype(BF16))
            both = jnp.concatenate(
                [source32[pl.ds(k, 8, stride=128), :], source32[pl.ds(KP + k, 8, stride=128), :]], 0
            )
            lhs.append(
                jnp.concatenate([jnp.where(first_half, both, 0.0), jnp.where(first_half, 0.0, both)], 0).astype(BF16)
            )
        return acc + dot_nt(jnp.concatenate(lhs, 1), jnp.concatenate(rhs, 1))

    both = lax.fori_loop(0, 7, contract, jnp.zeros((32, K), F32))
    both = jnp.concatenate([both, jnp.zeros((32, 128 - K), F32)], 1)
    coarse_local = jnp.concatenate(
        [both[0:8] + pltpu.roll(both[8:16], KP, 1), both[16:24] + pltpu.roll(both[24:32], KP, 1)], 0
    ).astype(BF16)
    tables = octant_tables(down, wide)
    for o in range(8):
        mid = dot_nt(coarse_local, tables[o])
        mid32[o * 8 : o * 8 + 8, :] = mid[:8]
        mid32[64 + o * 8 : 64 + o * 8 + 8, :] = mid[8:]
    mids = mid32[...].astype(BF16)
    for o in range(8):
        part = dot_nt(mids, tables[o])
        for m in range(16):
            local32[m * 64 + o * 8 : m * 64 + o * 8 + 8, :] = part[m * 8 : m * 8 + 8]

    lax.fori_loop(0, 2, finish, 0)

    def block_and_finish(tb, carry):
        block(tb, 0)
        finish(tb, 0)
        return carry

    lax.fori_loop(2, 4, block_and_finish, 0)

    def chan_wait(tb, carry):
        for d in range(1, CHANS):
            chan_copy(tb, d, chan).wait_send()
            chan_copy(tb, d, lax.rem(chan + CHANS - d, CHANS)).wait_recv()
        return carry

    lax.fori_loop(0, 4, chan_wait, 0)


def field_kernel(harm, leaf, local, wide_mix, out, acc, mixed):
    acc[...] = jnp.zeros_like(acc)
    for dev in range(4):
        def mix(i, carry):
            cols = pl.ds(pl.multiple_of(i * 512, 512), 512)
            weight = wide_mix[:, pl.ds(pl.multiple_of(dev * 1024 + i * 512, 512), 512)].astype(F32)
            lane = lax.rem(lax.broadcasted_iota(jnp.int32, (16, 512), 1), KP)
            lhs = jnp.concatenate([jnp.where(lane == q, weight, 0.0).astype(BF16) for q in range(K)], 0)
            acc[...] += dot_nt(lhs, local[dev, :, cols])
            return carry

        lax.fori_loop(0, 2, mix, 0)
    mixed[...] = acc[...].astype(BF16)
    step = 256

    def turn(i, carry):
        at = pl.ds(pl.multiple_of(i * step, step), step)
        onehot = jnp.where(
            leaf[:, at] == lax.broadcasted_iota(jnp.int32, (LB, step), 0), 1.0, 0.0
        ).astype(BF16)
        picked = jnp.dot(mixed[...], onehot, preferred_element_type=F32)
        h = harm[:, at].astype(F32)
        total = jnp.zeros((CH, step), F32)
        for q in range(K):
            total += h[q : q + 1] * picked[q * 16 : q * 16 + 16]
        out[:, at] = total.astype(BF16)
        return carry

    lax.fori_loop(0, ATOMS // step, turn, 0)


def on_device(
    features, harmonics, atom_leaf, leaf_sources, coarse_sources, coarse_class,
    child_to_parent, parent_to_child, leaf_transfer, coarse_transfer, mix_weight,
):
    params = dict(vmem_limit_bytes=60 << 20)
    leaf_row = atom_leaf.reshape(1, ATOMS)
    local_all = pl.pallas_call(
        far_kernel,
        out_shape=jax.ShapeDtypeStruct((CHANS, LB, 1024), BF16),
        in_specs=[VMEM] * 8 + [ANY] * 2,
        out_specs=VMEM,
        scratch_shapes=[
            pltpu.VMEM((KP, ATOMS), BF16),
            pltpu.VMEM((LB, 1024), F32),
            pltpu.VMEM((1024, 128), F32),
            pltpu.VMEM((1024, 128), BF16),
            pltpu.VMEM((1024, 128), BF16),
            pltpu.VMEM((1024, 128), BF16),
            pltpu.VMEM((128, 128), F32),
            pltpu.VMEM((KP * 8, 128), F32),
            pltpu.VMEM((BOXES * 16, 128), BF16),
            pltpu.VMEM((K, K, SLOTS), BF16),
            pltpu.VMEM((K, K, CLASSES), BF16),
            pltpu.VMEM((128 * 192, 128), F32),
            pltpu.VMEM((192, 128, 128), BF16),
            pltpu.VMEM((24, 8, 128), I32),
            pltpu.SMEM((24, 8, 128), I32),
            pltpu.VMEM((EMPTY + 8, 128), F32),
            pltpu.VMEM((1024, 128), F32),
            pltpu.VMEM((1024, 128), F32),
            pltpu.VMEM((K * 56, 128), F32),
            pltpu.VMEM((1024, 128), F32),
            pltpu.SemaphoreType.DMA((2,)),
            pltpu.SemaphoreType.DMA,
            pltpu.SemaphoreType.DMA((2,)),
            pltpu.SemaphoreType.DMA((2,)),
            pltpu.SemaphoreType.DMA((BOXES,)),
            pltpu.SemaphoreType.DMA((BOXES,)),
            pltpu.SemaphoreType.DMA((4, CHANS)),
            pltpu.SemaphoreType.DMA((4, CHANS)),
        ],
        compiler_params=pltpu.CompilerParams(collective_id=0, has_side_effects=True, **params),
        name="far",
    )(
        features, harmonics, leaf_row, leaf_sources.T, coarse_sources, coarse_class,
        child_to_parent.transpose(1, 0, 2), parent_to_child.transpose(1, 0, 2),
        leaf_transfer.transpose(1, 2, 0), coarse_transfer.transpose(1, 2, 0),
    )

    start = lax.axis_index("chan") * CH
    mine = lax.dynamic_slice_in_dim(mix_weight, start, CH, 1)
    wide = jnp.pad(mine[DEGREE], ((0, KP - K), (0, 0), (0, 0)))
    wide = wide.transpose(1, 2, 0).reshape(CH, 64 * KP)
    return pl.pallas_call(
        field_kernel,
        out_shape=jax.ShapeDtypeStruct((CH, ATOMS), BF16),
        in_specs=[VMEM] * 4,
        out_specs=VMEM,
        scratch_shapes=[pltpu.VMEM((K * 16, 128), F32), pltpu.VMEM((K * 16, 128), BF16)],
        compiler_params=pltpu.CompilerParams(**params),
        name="field",
    )(harmonics, leaf_row, local_all, wide)


def solution(mesh):
    placed = (
        P("chan", "box"), P(None, "box"), P("box"), P("box", None), P("box", None), P("box", None),
        P(), P(), P(), P(), P(),
    )
    return jax.shard_map(
        on_device, mesh=mesh, in_specs=placed, out_specs=P("chan", "box"), check_vma=False
    )
```

```python
import jax
import jax.numpy as jnp
import numpy as np
from jax import lax
from jax.experimental import pallas as pl
from jax.experimental.pallas import tpu as pltpu
from jax.sharding import PartitionSpec as P

F32 = jnp.float32
BF16 = jnp.bfloat16
I32 = jnp.int32
MESH = pl.DeviceIdType.MESH
K = 49
KP = 64
CH = 16
CP = 8
LB = 128
ATOMS = 8192
SLOTS = 189
CLASSES = 316
BOXES = 64
CHANS = 4
EMPTY = 3 * LB * CP
NT = (((1,), (1,)), ((), ()))
VMEM = pl.BlockSpec(memory_space=pltpu.VMEM)
ANY = pl.BlockSpec(memory_space=pl.ANY)
DEGREE = np.array([int(np.sqrt(k)) for k in range(K)])


def dot_nt(a, b):
    return lax.dot_general(a, b, NT, preferred_element_type=F32)


def below(block, rows):
    return jnp.concatenate([block, jnp.zeros((rows - block.shape[0], block.shape[1]), block.dtype)], 0)


def octant_tables(ref, wide):
    wide[...] = jnp.zeros_like(wide)
    wide[0 : K * 8, 0:K] = ref[...].astype(F32).reshape(K * 8, K)
    tables = []
    for o in range(8):
        part = wide[pl.ds(o, KP, stride=8), :]
        tables.append(jnp.concatenate([part, pltpu.roll(part, KP, 1)], 0).astype(BF16))
    return tables


def onehot_rows(row, count):
    shape = (count, row.shape[1])
    return jnp.where(row == lax.broadcasted_iota(I32, shape, 0), 1.0, 0.0).astype(BF16)


def far_kernel(
    feat, harm, leaf, sources, csource, cclass, up, down, transfer, ctransfer,
    out,
    hpad, acc, own32, own, before, after, mid32, wide, call, transfer_v, ctransfer_v, byrow, weights,
    index_v, index_s, table, far32, local32, picked32, source32,
    load_sem, index_sem, halo_send, halo_recv, call_send, call_recv, chan_send, chan_recv,
):
    box = lax.axis_index("box")
    chan = lax.axis_index("chan")
    load_a = pltpu.make_async_copy(transfer, transfer_v, load_sem.at[0])
    load_b = pltpu.make_async_copy(ctransfer, ctransfer_v, load_sem.at[1])
    load_a.start()
    load_b.start()
    barrier = pltpu.get_barrier_semaphore()

    def greet(d, carry):
        pl.semaphore_signal(
            barrier, inc=1, device_id={"box": lax.rem(box + d, BOXES)}, device_id_type=MESH
        )
        return carry

    lax.fori_loop(1, BOXES, greet, 0)
    for d in range(1, CHANS):
        pl.semaphore_signal(
            barrier, inc=1, device_id={"chan": lax.rem(chan + d, CHANS)}, device_id_type=MESH
        )

    step = 512
    hpad[...] = below(harm[...].astype(F32), KP).astype(BF16)
    acc[...] = jnp.zeros_like(acc)

    def turn(i, carry):
        at = pl.ds(pl.multiple_of(i * step, step), step)
        onehot = onehot_rows(leaf[:, at], LB)
        h = hpad[:, at]
        f = feat[:, at]
        for group in range(4):
            products = jnp.concatenate([h * f[4 * group + c : 4 * group + c + 1] for c in range(4)], 0)
            cols = slice(group * 256, group * 256 + 256)
            acc[:, cols] += dot_nt(onehot, products)
        return carry

    lax.fori_loop(0, ATOMS // step, turn, 0)
    for pair in range(CP):
        part = acc[:, pair * 128 : pair * 128 + 128].astype(BF16).astype(F32)
        own32[pl.ds(pair, LB, stride=CP), :] = part
    own[...] = own32[...].astype(BF16)

    pl.semaphore_wait(barrier, BOXES - 1 + CHANS - 1)
    right = {"box": lax.rem(box + 1, BOXES)}
    left = {"box": lax.rem(box + BOXES - 1, BOXES)}
    halos = [
        pltpu.make_async_remote_copy(
            src_ref=own, dst_ref=slot, send_sem=halo_send.at[i], recv_sem=halo_recv.at[i],
            device_id=where, device_id_type=MESH,
        )
        for i, (slot, where) in enumerate(((before, right), (after, left)))
    ]
    for copy in halos:
        copy.start()

    tables = octant_tables(up, wide)
    children = own32[...].reshape(16, 8, CP, 128)
    mid = jnp.zeros((128, 128), F32)
    for o in range(8):
        mid += dot_nt(children[:, o].reshape(128, 128).astype(BF16), tables[o])
    mid32[...] = mid.astype(BF16).astype(F32)
    mids = mid32[...].reshape(2, 8, CP, 128)
    coarse = jnp.zeros((16, 128), F32)
    for o in range(8):
        coarse += dot_nt(mids[:, o].reshape(16, 128).astype(BF16), tables[o])
    mine = call.at[pl.ds(pl.multiple_of(box * 16, 16), 16)]
    mine[...] = coarse.astype(BF16)

    def call_copy(d, sender):
        rows = call.at[pl.ds(pl.multiple_of(sender * 16, 16), 16)]
        return pltpu.make_async_remote_copy(
            src_ref=rows, dst_ref=rows, send_sem=call_send.at[d], recv_sem=call_recv.at[sender],
            device_id={"box": lax.rem(box + d, BOXES)}, device_id_type=MESH,
        )

    def call_start(d, carry):
        call_copy(d, box).start()
        return carry

    lax.fori_loop(1, BOXES, call_start, 0)

    rows = jnp.clip((sources[...] - (box * LB - LB)) * CP, 0, EMPTY - CP)
    rows = jnp.where(sources[...] >= 0, rows, EMPTY)
    index_v[...] = jnp.concatenate([rows, jnp.full((192 - SLOTS, LB), EMPTY, I32)], 0)
    index_copy = pltpu.make_async_copy(index_v, index_s, index_sem)
    index_copy.start()

    load_a.wait()
    for half in range(2):
        byrow[:, (half * KP + K) * 8 : (half + 1) * KP * 8, :] = jnp.zeros((24, (KP - K) * 8, 128), F32)
    eye = jnp.where(
        lax.broadcasted_iota(I32, (192, SLOTS), 0) == lax.broadcasted_iota(I32, (192, SLOTS), 1), 1.0, 0.0
    ).astype(BF16)

    def turn_slots(q, carry):
        block = below(transfer_v[q].astype(F32), KP).astype(BF16)
        gap = jnp.zeros((128, SLOTS), BF16)
        both = dot_nt(eye, jnp.concatenate([block, gap, block], 0))
        byrow[:, pl.ds(pl.multiple_of(q * 8, 8), 8), :] = both[:, :128].reshape(24, 8, 128)
        byrow[:, pl.ds(pl.multiple_of((KP + q) * 8, 8), 8), :] = both[:, 128:].reshape(24, 8, 128)
        return carry

    lax.fori_loop(0, K, turn_slots, 0)

    def pack_slots(g, carry):
        for r in range(8):
            weights[g * 8 + r] = byrow[g, pl.ds(r, 128, stride=8), :].astype(BF16)
        return carry

    lax.fori_loop(0, 24, pack_slots, 0)

    load_b.wait()
    class_row = jnp.concatenate([cclass[0:1, :], cclass[1:2, :]], 1)
    class_hot = onehot_rows(class_row, CLASSES)

    def pick_classes(i, carry):
        blocks = [below(ctransfer_v[i * 7 + r].astype(F32), 56).astype(BF16) for r in range(7)]
        picked32[pl.ds(pl.multiple_of(i * 392, 8), 392), :] = jnp.dot(
            jnp.concatenate(blocks, 0), class_hot, preferred_element_type=F32
        )
        return carry

    lax.fori_loop(0, 7, pick_classes, 0)
    index_copy.wait()

    table[1024:2048, :] = own32[...]
    table[3072:3080, :] = jnp.zeros((8, 128), F32)
    for copy in halos:
        copy.wait()
    table[0:1024, :] = before[...].astype(F32)
    table[2048:3072, :] = after[...].astype(F32)

    def block(tb, carry):
        def chunk(jc, acc):
            def pick(jj, t):
                row = index_s.at[pl.ds(jj, 161), pl.ds(t, 97)][jc * 32, tb * 32]
                return table[pl.ds(row, 8), :]

            parts = []
            for jj in range(32):
                pairs = [
                    jnp.concatenate([pick(jj, t), pick(jj, t + 1)], 0).astype(BF16) for t in range(0, 32, 2)
                ]
                parts.append(jnp.concatenate(pairs, 0))
            lhs = jnp.concatenate(parts, 1)
            rhs = jnp.concatenate([weights[jc * 32 + jj] for jj in range(32)], 1)
            return acc + dot_nt(lhs, rhs)

        total = lax.fori_loop(0, 6, chunk, jnp.zeros((256, 128), F32))
        far32[pl.ds(pl.multiple_of(tb * 256, 256), 256), :] = total
        return carry

    def chan_copy(tb, d, sender):
        part = out.at[sender, pl.ds(pl.multiple_of(tb * 32, 32), 32)]
        return pltpu.make_async_remote_copy(
            src_ref=part, dst_ref=part, send_sem=chan_send.at[tb, d], recv_sem=chan_recv.at[tb, sender],
            device_id={"chan": lax.rem(chan + d, CHANS)}, device_id_type=MESH,
        )

    def finish(tb, carry):
        rows = pl.ds(pl.multiple_of(tb * 256, 256), 256)
        far32[rows, :] += local32[rows, :]
        for pair in range(CP):
            part = far32[pl.ds(tb * 256 + pair, 32, stride=CP), :]
            out[chan, pl.ds(pl.multiple_of(tb * 32, 32), 32), pair * 128 : pair * 128 + 128] = part.astype(BF16)
        for d in range(1, CHANS):
            chan_copy(tb, d, chan).start()
        return carry

    lax.fori_loop(0, 2, block, 0)

    def call_wait(d, carry):
        call_copy(d, box).wait_send()
        call_copy(d, lax.rem(box + BOXES - d, BOXES)).wait_recv()
        return carry

    lax.fori_loop(1, BOXES, call_wait, 0)
    source_row = jnp.concatenate([csource[0:1, :], csource[1:2, :]], 1)
    source_hot = onehot_rows(source_row, 128)
    own32[...] = call[...].astype(F32)
    for pair in range(CP):
        flat = own32[pl.ds(pair, 128, stride=CP), :].T.astype(BF16)
        source32[pair * 128 : pair * 128 + 128, :] = jnp.dot(flat, source_hot, preferred_element_type=F32)
    first_half = lax.broadcasted_iota(I32, (16, 128), 1) < KP

    def contract(i, acc):
        lhs, rhs = [], []
        for r in range(7):
            k = i * 7 + r
            rhs.append(picked32[pl.ds(k, K, stride=56), :].astype(BF16))
            both = jnp.concatenate(
                [source32[pl.ds(k, 8, stride=128), :], source32[pl.ds(KP + k, 8, stride=128), :]], 0
            )
            lhs.append(
                jnp.concatenate([jnp.where(first_half, both, 0.0), jnp.where(first_half, 0.0, both)], 0).astype(BF16)
            )
        return acc + dot_nt(jnp.concatenate(lhs, 1), jnp.concatenate(rhs, 1))

    both = lax.fori_loop(0, 7, contract, jnp.zeros((32, K), F32))
    both = jnp.concatenate([both, jnp.zeros((32, 128 - K), F32)], 1)
    coarse_local = jnp.concatenate(
        [both[0:8] + pltpu.roll(both[8:16], KP, 1), both[16:24] + pltpu.roll(both[24:32], KP, 1)], 0
    ).astype(BF16)
    tables = octant_tables(down, wide)
    for o in range(8):
        mid = dot_nt(coarse_local, tables[o])
        mid32[o * 8 : o * 8 + 8, :] = mid[:8]
        mid32[64 + o * 8 : 64 + o * 8 + 8, :] = mid[8:]
    mids = mid32[...].astype(BF16)
    for o in range(8):
        part = dot_nt(mids, tables[o])
        for m in range(16):
            local32[m * 64 + o * 8 : m * 64 + o * 8 + 8, :] = part[m * 8 : m * 8 + 8]

    lax.fori_loop(0, 2, finish, 0)

    def block_and_finish(tb, carry):
        block(tb, 0)
        finish(tb, 0)
        return carry

    lax.fori_loop(2, 4, block_and_finish, 0)

    def chan_wait(tb, carry):
        for d in range(1, CHANS):
            chan_copy(tb, d, chan).wait_send()
            chan_copy(tb, d, lax.rem(chan + CHANS - d, CHANS)).wait_recv()
        return carry

    lax.fori_loop(0, 4, chan_wait, 0)


def field_kernel(harm, leaf, local, wide_mix, out, acc, mixed):
    acc[...] = jnp.zeros_like(acc)
    for dev in range(4):
        def mix(i, carry):
            cols = pl.ds(pl.multiple_of(i * 512, 512), 512)
            weight = wide_mix[:, pl.ds(pl.multiple_of(dev * 1024 + i * 512, 512), 512)].astype(F32)
            lane = lax.rem(lax.broadcasted_iota(jnp.int32, (16, 512), 1), KP)
            lhs = jnp.concatenate([jnp.where(lane == q, weight, 0.0).astype(BF16) for q in range(K)], 0)
            acc[...] += dot_nt(lhs, local[dev, :, cols])
            return carry

        lax.fori_loop(0, 2, mix, 0)
    mixed[...] = acc[...].astype(BF16)
    step = 512

    def turn(i, carry):
        at = pl.ds(pl.multiple_of(i * step, step), step)
        onehot = jnp.where(
            leaf[:, at] == lax.broadcasted_iota(jnp.int32, (LB, step), 0), 1.0, 0.0
        ).astype(BF16)
        picked = jnp.dot(mixed[...], onehot, preferred_element_type=F32)
        h = harm[:, at].astype(F32)
        total = jnp.zeros((CH, step), F32)
        for q in range(K):
            total += h[q : q + 1] * picked[q * 16 : q * 16 + 16]
        out[:, at] = total.astype(BF16)
        return carry

    lax.fori_loop(0, ATOMS // step, turn, 0)


def on_device(
    features, harmonics, atom_leaf, leaf_sources, coarse_sources, coarse_class,
    child_to_parent, parent_to_child, leaf_transfer, coarse_transfer, mix_weight,
):
    params = dict(vmem_limit_bytes=60 << 20)
    leaf_row = atom_leaf.reshape(1, ATOMS)
    local_all = pl.pallas_call(
        far_kernel,
        out_shape=jax.ShapeDtypeStruct((CHANS, LB, 1024), BF16),
        in_specs=[VMEM] * 8 + [ANY] * 2,
        out_specs=VMEM,
        scratch_shapes=[
            pltpu.VMEM((KP, ATOMS), BF16),
            pltpu.VMEM((LB, 1024), F32),
            pltpu.VMEM((1024, 128), F32),
            pltpu.VMEM((1024, 128), BF16),
            pltpu.VMEM((1024, 128), BF16),
            pltpu.VMEM((1024, 128), BF16),
            pltpu.VMEM((128, 128), F32),
            pltpu.VMEM((KP * 8, 128), F32),
            pltpu.VMEM((BOXES * 16, 128), BF16),
            pltpu.VMEM((K, K, SLOTS), BF16),
            pltpu.VMEM((K, K, CLASSES), BF16),
            pltpu.VMEM((24, 1024, 128), F32),
            pltpu.VMEM((192, 128, 128), BF16),
            pltpu.VMEM((192, LB), I32),
            pltpu.SMEM((192, LB), I32),
            pltpu.VMEM((EMPTY + 8, 128), F32),
            pltpu.VMEM((1024, 128), F32),
            pltpu.VMEM((1024, 128), F32),
            pltpu.VMEM((K * 56, 128), F32),
            pltpu.VMEM((1024, 128), F32),
            pltpu.SemaphoreType.DMA((2,)),
            pltpu.SemaphoreType.DMA,
            pltpu.SemaphoreType.DMA((2,)),
            pltpu.SemaphoreType.DMA((2,)),
            pltpu.SemaphoreType.DMA((BOXES,)),
            pltpu.SemaphoreType.DMA((BOXES,)),
            pltpu.SemaphoreType.DMA((4, CHANS)),
            pltpu.SemaphoreType.DMA((4, CHANS)),
        ],
        compiler_params=pltpu.CompilerParams(collective_id=0, has_side_effects=True, **params),
        name="far",
    )(
        features, harmonics, leaf_row, leaf_sources.T, coarse_sources, coarse_class,
        child_to_parent.transpose(1, 0, 2), parent_to_child.transpose(1, 0, 2),
        leaf_transfer.transpose(1, 2, 0), coarse_transfer.transpose(1, 2, 0),
    )

    start = lax.axis_index("chan") * CH
    mine = lax.dynamic_slice_in_dim(mix_weight, start, CH, 1)
    wide = jnp.pad(mine[DEGREE], ((0, KP - K), (0, 0), (0, 0)))
    wide = wide.transpose(1, 2, 0).reshape(CH, 64 * KP)
    return pl.pallas_call(
        field_kernel,
        out_shape=jax.ShapeDtypeStruct((CH, ATOMS), BF16),
        in_specs=[VMEM] * 4,
        out_specs=VMEM,
        scratch_shapes=[pltpu.VMEM((K * 16, 128), F32), pltpu.VMEM((K * 16, 128), BF16)],
        compiler_params=pltpu.CompilerParams(**params),
        name="field",
    )(harmonics, leaf_row, local_all, wide)


def solution(mesh):
    placed = (
        P("chan", "box"), P(None, "box"), P("box"), P("box", None), P("box", None), P("box", None),
        P(), P(), P(), P(), P(),
    )
    return jax.shard_map(
        on_device, mesh=mesh, in_specs=placed, out_specs=P("chan", "box"), check_vma=False
    )
```

```python
import jax
import jax.numpy as jnp
import numpy as np
from jax import lax
from jax.experimental import pallas as pl
from jax.experimental.pallas import tpu as pltpu
from jax.sharding import PartitionSpec as P

F32 = jnp.float32
BF16 = jnp.bfloat16
I32 = jnp.int32
MESH = pl.DeviceIdType.MESH
K = 49
KP = 64
CH = 16
CP = 8
LB = 128
ATOMS = 8192
SLOTS = 189
CLASSES = 316
BOXES = 64
CHANS = 4
EMPTY = 3 * LB * CP
NT = (((1,), (1,)), ((), ()))
VMEM = pl.BlockSpec(memory_space=pltpu.VMEM)
ANY = pl.BlockSpec(memory_space=pl.ANY)
DEGREE = np.array([int(np.sqrt(k)) for k in range(K)])


def dot_nt(a, b):
    return lax.dot_general(a, b, NT, preferred_element_type=F32)


def below(block, rows):
    return jnp.concatenate([block, jnp.zeros((rows - block.shape[0], block.shape[1]), block.dtype)], 0)


def octant_tables(ref, wide):
    wide[...] = jnp.zeros_like(wide)
    wide[0 : K * 8, 0:K] = ref[...].astype(F32).reshape(K * 8, K)
    tables = []
    for o in range(8):
        part = wide[pl.ds(o, KP, stride=8), :]
        tables.append(jnp.concatenate([part, pltpu.roll(part, KP, 1)], 0).astype(BF16))
    return tables


def onehot_rows(row, count):
    shape = (count, row.shape[1])
    return jnp.where(row == lax.broadcasted_iota(I32, shape, 0), 1.0, 0.0).astype(BF16)


def far_kernel(
    feat, harm, leaf, sources, csource, cclass, up, down, transfer, ctransfer,
    out,
    hpad, acc, own32, own, before, after, mid32, wide, call, transfer_v, ctransfer_v, byrow, weights,
    index_v, index_s, table, far32, local32, picked32, source32,
    load_sem, index_sem, halo_send, halo_recv, call_send, call_recv, chan_send, chan_recv,
):
    box = lax.axis_index("box")
    chan = lax.axis_index("chan")
    load_a = pltpu.make_async_copy(transfer, transfer_v, load_sem.at[0])
    load_b = pltpu.make_async_copy(ctransfer, ctransfer_v, load_sem.at[1])
    load_a.start()
    load_b.start()
    barrier = pltpu.get_barrier_semaphore()

    def greet(d, carry):
        pl.semaphore_signal(
            barrier, inc=1, device_id={"box": lax.rem(box + d, BOXES)}, device_id_type=MESH
        )
        return carry

    lax.fori_loop(1, BOXES, greet, 0)
    for d in range(1, CHANS):
        pl.semaphore_signal(
            barrier, inc=1, device_id={"chan": lax.rem(chan + d, CHANS)}, device_id_type=MESH
        )

    step = 1024
    hpad[...] = below(harm[...].astype(F32), KP).astype(BF16)
    acc[...] = jnp.zeros_like(acc)

    def turn(i, carry):
        at = pl.ds(pl.multiple_of(i * step, step), step)
        onehot = onehot_rows(leaf[:, at], LB)
        h = hpad[:, at]
        f = feat[:, at]
        for group in range(4):
            products = jnp.concatenate([h * f[4 * group + c : 4 * group + c + 1] for c in range(4)], 0)
            cols = slice(group * 256, group * 256 + 256)
            acc[:, cols] += dot_nt(onehot, products)
        return carry

    lax.fori_loop(0, ATOMS // step, turn, 0)
    for pair in range(CP):
        part = acc[:, pair * 128 : pair * 128 + 128].astype(BF16).astype(F32)
        own32[pl.ds(pair, LB, stride=CP), :] = part
    own[...] = own32[...].astype(BF16)

    pl.semaphore_wait(barrier, BOXES - 1 + CHANS - 1)
    right = {"box": lax.rem(box + 1, BOXES)}
    left = {"box": lax.rem(box + BOXES - 1, BOXES)}
    halos = [
        pltpu.make_async_remote_copy(
            src_ref=own, dst_ref=slot, send_sem=halo_send.at[i], recv_sem=halo_recv.at[i],
            device_id=where, device_id_type=MESH,
        )
        for i, (slot, where) in enumerate(((before, right), (after, left)))
    ]
    for copy in halos:
        copy.start()

    tables = octant_tables(up, wide)
    children = own32[...].reshape(16, 8, CP, 128)
    mid = jnp.zeros((128, 128), F32)
    for o in range(8):
        mid += dot_nt(children[:, o].reshape(128, 128).astype(BF16), tables[o])
    mid32[...] = mid.astype(BF16).astype(F32)
    mids = mid32[...].reshape(2, 8, CP, 128)
    coarse = jnp.zeros((16, 128), F32)
    for o in range(8):
        coarse += dot_nt(mids[:, o].reshape(16, 128).astype(BF16), tables[o])
    mine = call.at[pl.ds(pl.multiple_of(box * 16, 16), 16)]
    mine[...] = coarse.astype(BF16)

    def call_copy(d, sender):
        rows = call.at[pl.ds(pl.multiple_of(sender * 16, 16), 16)]
        return pltpu.make_async_remote_copy(
            src_ref=rows, dst_ref=rows, send_sem=call_send.at[d], recv_sem=call_recv.at[sender],
            device_id={"box": lax.rem(box + d, BOXES)}, device_id_type=MESH,
        )

    def call_start(d, carry):
        call_copy(d, box).start()
        return carry

    lax.fori_loop(1, BOXES, call_start, 0)

    rows = jnp.clip((sources[...] - (box * LB - LB)) * CP, 0, EMPTY - CP)
    rows = jnp.where(sources[...] >= 0, rows, EMPTY)
    index_v[...] = jnp.concatenate([rows, jnp.full((192 - SLOTS, LB), EMPTY, I32)], 0)
    index_copy = pltpu.make_async_copy(index_v, index_s, index_sem)
    index_copy.start()

    load_a.wait()
    for half in range(2):
        byrow[:, (half * KP + K) * 8 : (half + 1) * KP * 8, :] = jnp.zeros((24, (KP - K) * 8, 128), F32)
    eye = jnp.where(
        lax.broadcasted_iota(I32, (192, SLOTS), 0) == lax.broadcasted_iota(I32, (192, SLOTS), 1), 1.0, 0.0
    ).astype(BF16)

    def turn_slots(i, carry):
        gap = jnp.zeros((128, SLOTS), BF16)
        for r in range(7):
            q = i * 7 + r
            block = below(transfer_v[q].astype(F32), KP).astype(BF16)
            both = dot_nt(eye, jnp.concatenate([block, gap, block], 0))
            byrow[:, pl.ds(pl.multiple_of(q * 8, 8), 8), :] = both[:, :128].reshape(24, 8, 128)
            byrow[:, pl.ds(pl.multiple_of((KP + q) * 8, 8), 8), :] = both[:, 128:].reshape(24, 8, 128)
        return carry

    lax.fori_loop(0, 7, turn_slots, 0)

    def pack_slots(g, carry):
        for r in range(8):
            weights[g * 8 + r] = byrow[g, pl.ds(r, 128, stride=8), :].astype(BF16)
        return carry

    lax.fori_loop(0, 24, pack_slots, 0)

    load_b.wait()
    class_row = jnp.concatenate([cclass[0:1, :], cclass[1:2, :]], 1)
    class_hot = onehot_rows(class_row, CLASSES)

    def pick_classes(i, carry):
        blocks = [below(ctransfer_v[i * 7 + r].astype(F32), 56).astype(BF16) for r in range(7)]
        picked32[pl.ds(pl.multiple_of(i * 392, 8), 392), :] = jnp.dot(
            jnp.concatenate(blocks, 0), class_hot, preferred_element_type=F32
        )
        return carry

    lax.fori_loop(0, 7, pick_classes, 0)
    index_copy.wait()

    table[1024:2048, :] = own32[...]
    table[3072:3080, :] = jnp.zeros((8, 128), F32)
    for copy in halos:
        copy.wait()
    table[0:1024, :] = before[...].astype(F32)
    table[2048:3072, :] = after[...].astype(F32)

    def block(tb, carry):
        def chunk(jc, acc):
            def pick(jj, t):
                row = index_s.at[pl.ds(jj, 129), pl.ds(t, 97)][jc * 64, tb * 32]
                return table[pl.ds(row, 8), :]

            parts = []
            for jj in range(64):
                pairs = [
                    jnp.concatenate([pick(jj, t), pick(jj, t + 1)], 0).astype(BF16) for t in range(0, 32, 2)
                ]
                parts.append(jnp.concatenate(pairs, 0))
            lhs = jnp.concatenate(parts, 1)
            rhs = jnp.concatenate([weights[jc * 64 + jj] for jj in range(64)], 1)
            return acc + dot_nt(lhs, rhs)

        total = lax.fori_loop(0, 3, chunk, jnp.zeros((256, 128), F32))
        far32[pl.ds(pl.multiple_of(tb * 256, 256), 256), :] = total
        return carry

    def chan_copy(tb, d, sender):
        part = out.at[sender, pl.ds(pl.multiple_of(tb * 32, 32), 32)]
        return pltpu.make_async_remote_copy(
            src_ref=part, dst_ref=part, send_sem=chan_send.at[tb, d], recv_sem=chan_recv.at[tb, sender],
            device_id={"chan": lax.rem(chan + d, CHANS)}, device_id_type=MESH,
        )

    def finish(tb, carry):
        rows = pl.ds(pl.multiple_of(tb * 256, 256), 256)
        far32[rows, :] += local32[rows, :]
        for pair in range(CP):
            part = far32[pl.ds(tb * 256 + pair, 32, stride=CP), :]
            out[chan, pl.ds(pl.multiple_of(tb * 32, 32), 32), pair * 128 : pair * 128 + 128] = part.astype(BF16)
        for d in range(1, CHANS):
            chan_copy(tb, d, chan).start()
        return carry

    lax.fori_loop(0, 2, block, 0)

    def call_wait(d, carry):
        call_copy(d, box).wait_send()
        call_copy(d, lax.rem(box + BOXES - d, BOXES)).wait_recv()
        return carry

    lax.fori_loop(1, BOXES, call_wait, 0)
    source_row = jnp.concatenate([csource[0:1, :], csource[1:2, :]], 1)
    source_hot = onehot_rows(source_row, 128)
    own32[...] = call[...].astype(F32)
    for pair in range(CP):
        flat = own32[pl.ds(pair, 128, stride=CP), :].T.astype(BF16)
        source32[pair * 128 : pair * 128 + 128, :] = jnp.dot(flat, source_hot, preferred_element_type=F32)
    first_half = lax.broadcasted_iota(I32, (16, 128), 1) < KP

    def contract(i, acc):
        lhs, rhs = [], []
        for r in range(7):
            k = i * 7 + r
            rhs.append(picked32[pl.ds(k, K, stride=56), :].astype(BF16))
            both = jnp.concatenate(
                [source32[pl.ds(k, 8, stride=128), :], source32[pl.ds(KP + k, 8, stride=128), :]], 0
            )
            lhs.append(
                jnp.concatenate([jnp.where(first_half, both, 0.0), jnp.where(first_half, 0.0, both)], 0).astype(BF16)
            )
        return acc + dot_nt(jnp.concatenate(lhs, 1), jnp.concatenate(rhs, 1))

    both = lax.fori_loop(0, 7, contract, jnp.zeros((32, K), F32))
    both = jnp.concatenate([both, jnp.zeros((32, 128 - K), F32)], 1)
    coarse_local = jnp.concatenate(
        [both[0:8] + pltpu.roll(both[8:16], KP, 1), both[16:24] + pltpu.roll(both[24:32], KP, 1)], 0
    ).astype(BF16)
    tables = octant_tables(down, wide)
    for o in range(8):
        mid = dot_nt(coarse_local, tables[o])
        mid32[o * 8 : o * 8 + 8, :] = mid[:8]
        mid32[64 + o * 8 : 64 + o * 8 + 8, :] = mid[8:]
    mids = mid32[...].astype(BF16)
    for o in range(8):
        part = dot_nt(mids, tables[o])
        for m in range(16):
            local32[m * 64 + o * 8 : m * 64 + o * 8 + 8, :] = part[m * 8 : m * 8 + 8]

    lax.fori_loop(0, 2, finish, 0)

    def block_and_finish(tb, carry):
        block(tb, 0)
        finish(tb, 0)
        return carry

    lax.fori_loop(2, 4, block_and_finish, 0)

    def chan_wait(tb, carry):
        for d in range(1, CHANS):
            chan_copy(tb, d, chan).wait_send()
            chan_copy(tb, d, lax.rem(chan + CHANS - d, CHANS)).wait_recv()
        return carry

    lax.fori_loop(0, 4, chan_wait, 0)


def field_kernel(harm, leaf, local, wide_mix, out, acc, mixed):
    acc[...] = jnp.zeros_like(acc)
    for dev in range(4):
        def mix(i, carry):
            cols = pl.ds(pl.multiple_of(i * 512, 512), 512)
            weight = wide_mix[:, pl.ds(pl.multiple_of(dev * 1024 + i * 512, 512), 512)].astype(F32)
            lane = lax.rem(lax.broadcasted_iota(jnp.int32, (16, 512), 1), KP)
            lhs = jnp.concatenate([jnp.where(lane == q, weight, 0.0).astype(BF16) for q in range(K)], 0)
            acc[...] += dot_nt(lhs, local[dev, :, cols])
            return carry

        lax.fori_loop(0, 2, mix, 0)
    mixed[...] = acc[...].astype(BF16)
    step = 512

    def turn(i, carry):
        at = pl.ds(pl.multiple_of(i * step, step), step)
        onehot = jnp.where(
            leaf[:, at] == lax.broadcasted_iota(jnp.int32, (LB, step), 0), 1.0, 0.0
        ).astype(BF16)
        picked = jnp.dot(mixed[...], onehot, preferred_element_type=F32)
        h = harm[:, at].astype(F32)
        total = jnp.zeros((CH, step), F32)
        for q in range(K):
            total += h[q : q + 1] * picked[q * 16 : q * 16 + 16]
        out[:, at] = total.astype(BF16)
        return carry

    lax.fori_loop(0, ATOMS // step, turn, 0)


def on_device(
    features, harmonics, atom_leaf, leaf_sources, coarse_sources, coarse_class,
    child_to_parent, parent_to_child, leaf_transfer, coarse_transfer, mix_weight,
):
    params = dict(vmem_limit_bytes=60 << 20)
    leaf_row = atom_leaf.reshape(1, ATOMS)
    local_all = pl.pallas_call(
        far_kernel,
        out_shape=jax.ShapeDtypeStruct((CHANS, LB, 1024), BF16),
        in_specs=[VMEM] * 8 + [ANY] * 2,
        out_specs=VMEM,
        scratch_shapes=[
            pltpu.VMEM((KP, ATOMS), BF16),
            pltpu.VMEM((LB, 1024), F32),
            pltpu.VMEM((1024, 128), F32),
            pltpu.VMEM((1024, 128), BF16),
            pltpu.VMEM((1024, 128), BF16),
            pltpu.VMEM((1024, 128), BF16),
            pltpu.VMEM((128, 128), F32),
            pltpu.VMEM((KP * 8, 128), F32),
            pltpu.VMEM((BOXES * 16, 128), BF16),
            pltpu.VMEM((K, K, SLOTS), BF16),
            pltpu.VMEM((K, K, CLASSES), BF16),
            pltpu.VMEM((24, 1024, 128), F32),
            pltpu.VMEM((192, 128, 128), BF16),
            pltpu.VMEM((192, LB), I32),
            pltpu.SMEM((192, LB), I32),
            pltpu.VMEM((EMPTY + 8, 128), F32),
            pltpu.VMEM((1024, 128), F32),
            pltpu.VMEM((1024, 128), F32),
            pltpu.VMEM((K * 56, 128), F32),
            pltpu.VMEM((1024, 128), F32),
            pltpu.SemaphoreType.DMA((2,)),
            pltpu.SemaphoreType.DMA,
            pltpu.SemaphoreType.DMA((2,)),
            pltpu.SemaphoreType.DMA((2,)),
            pltpu.SemaphoreType.DMA((BOXES,)),
            pltpu.SemaphoreType.DMA((BOXES,)),
            pltpu.SemaphoreType.DMA((4, CHANS)),
            pltpu.SemaphoreType.DMA((4, CHANS)),
        ],
        compiler_params=pltpu.CompilerParams(collective_id=0, has_side_effects=True, **params),
        name="far",
    )(
        features, harmonics, leaf_row, leaf_sources.T, coarse_sources, coarse_class,
        child_to_parent.transpose(1, 0, 2), parent_to_child.transpose(1, 0, 2),
        leaf_transfer.transpose(1, 2, 0), coarse_transfer.transpose(1, 2, 0),
    )

    start = lax.axis_index("chan") * CH
    mine = lax.dynamic_slice_in_dim(mix_weight, start, CH, 1)
    wide = jnp.pad(mine[DEGREE], ((0, KP - K), (0, 0), (0, 0)))
    wide = wide.transpose(1, 2, 0).reshape(CH, 64 * KP)
    return pl.pallas_call(
        field_kernel,
        out_shape=jax.ShapeDtypeStruct((CH, ATOMS), BF16),
        in_specs=[VMEM] * 4,
        out_specs=VMEM,
        scratch_shapes=[pltpu.VMEM((K * 16, 128), F32), pltpu.VMEM((K * 16, 128), BF16)],
        compiler_params=pltpu.CompilerParams(**params),
        name="field",
    )(harmonics, leaf_row, local_all, wide)


def solution(mesh):
    placed = (
        P("chan", "box"), P(None, "box"), P("box"), P("box", None), P("box", None), P("box", None),
        P(), P(), P(), P(), P(),
    )
    return jax.shard_map(
        on_device, mesh=mesh, in_specs=placed, out_specs=P("chan", "box"), check_vma=False
    )
```

```python
import jax
import jax.numpy as jnp
import numpy as np
from jax import lax
from jax.experimental import pallas as pl
from jax.experimental.pallas import tpu as pltpu
from jax.sharding import PartitionSpec as P

F32 = jnp.float32
BF16 = jnp.bfloat16
I32 = jnp.int32
MESH = pl.DeviceIdType.MESH
K = 49
KP = 64
CH = 16
CP = 8
LB = 128
ATOMS = 8192
SLOTS = 189
CLASSES = 316
BOXES = 64
CHANS = 4
EMPTY = 3 * LB * CP
NT = (((1,), (1,)), ((), ()))
VMEM = pl.BlockSpec(memory_space=pltpu.VMEM)
ANY = pl.BlockSpec(memory_space=pl.ANY)
DEG = 7
DEGREE = [int(np.sqrt(k)) for k in range(K)]


def dot_nt(a, b):
    return lax.dot_general(a, b, NT, preferred_element_type=F32)


def below(block, rows):
    return jnp.concatenate([block, jnp.zeros((rows - block.shape[0], block.shape[1]), block.dtype)], 0)


def octant_tables(ref, wide):
    wide[...] = jnp.zeros_like(wide)
    wide[0 : K * 8, 0:K] = ref[...].astype(F32).reshape(K * 8, K)
    tables = []
    for o in range(8):
        part = wide[pl.ds(o, KP, stride=8), :]
        tables.append(jnp.concatenate([part, pltpu.roll(part, KP, 1)], 0).astype(BF16))
    return tables


def onehot_rows(row, count):
    shape = (count, row.shape[1])
    return jnp.where(row == lax.broadcasted_iota(I32, shape, 0), 1.0, 0.0).astype(BF16)


def far_kernel(
    feat, harm, leaf, sources, csource, cclass, up, down, mix, transfer, ctransfer,
    out,
    local, acc, own32, own, before, after, mid32, wide, call, transfer_v, ctransfer_v, byrow, weights,
    index_v, index_s, table, far32, local32, picked32, source32,
    load_sem, index_sem, halo_send, halo_recv, call_send, call_recv, chan_send, chan_recv,
):
    box = lax.axis_index("box")
    chan = lax.axis_index("chan")
    load_a = pltpu.make_async_copy(transfer, transfer_v, load_sem.at[0])
    load_b = pltpu.make_async_copy(ctransfer, ctransfer_v, load_sem.at[1])
    load_a.start()
    load_b.start()
    barrier = pltpu.get_barrier_semaphore()

    def greet(d, carry):
        pl.semaphore_signal(
            barrier, inc=1, device_id={"box": lax.rem(box + d, BOXES)}, device_id_type=MESH
        )
        return carry

    lax.fori_loop(1, BOXES, greet, 0)
    for d in range(1, CHANS):
        pl.semaphore_signal(
            barrier, inc=1, device_id={"chan": lax.rem(chan + d, CHANS)}, device_id_type=MESH
        )

    step = 1024
    acc[...] = jnp.zeros_like(acc)

    def turn(i, carry):
        at = pl.ds(pl.multiple_of(i * step, step), step)
        h = harm[:, at]
        f = feat[:, at]
        products = jnp.concatenate([h[k : k + 1] * f for k in range(K)], 0)
        acc[0 : K * CH, :] += dot_nt(products, onehot_rows(leaf[:, at], LB))
        return carry

    lax.fori_loop(0, ATOMS // step, turn, 0)
    for pair in range(CP):
        both = jnp.concatenate([acc[pl.ds(2 * pair + p, KP, stride=CH), :] for p in range(2)], 0)
        own32[pl.ds(pair, LB, stride=CP), :] = both.T.astype(BF16).astype(F32)
    own[...] = own32[...].astype(BF16)

    pl.semaphore_wait(barrier, BOXES - 1 + CHANS - 1)
    right = {"box": lax.rem(box + 1, BOXES)}
    left = {"box": lax.rem(box + BOXES - 1, BOXES)}
    halos = [
        pltpu.make_async_remote_copy(
            src_ref=own, dst_ref=slot, send_sem=halo_send.at[i], recv_sem=halo_recv.at[i],
            device_id=where, device_id_type=MESH,
        )
        for i, (slot, where) in enumerate(((before, right), (after, left)))
    ]
    for copy in halos:
        copy.start()

    tables = octant_tables(up, wide)
    children = own32[...].reshape(16, 8, CP, 128)
    mid = jnp.zeros((128, 128), F32)
    for o in range(8):
        mid += dot_nt(children[:, o].reshape(128, 128).astype(BF16), tables[o])
    mid32[...] = mid.astype(BF16).astype(F32)
    mids = mid32[...].reshape(2, 8, CP, 128)
    coarse = jnp.zeros((16, 128), F32)
    for o in range(8):
        coarse += dot_nt(mids[:, o].reshape(16, 128).astype(BF16), tables[o])
    mine = call.at[pl.ds(pl.multiple_of(box * 16, 16), 16)]
    mine[...] = coarse.astype(BF16)

    def call_copy(d, sender):
        rows = call.at[pl.ds(pl.multiple_of(sender * 16, 16), 16)]
        return pltpu.make_async_remote_copy(
            src_ref=rows, dst_ref=rows, send_sem=call_send.at[d], recv_sem=call_recv.at[sender],
            device_id={"box": lax.rem(box + d, BOXES)}, device_id_type=MESH,
        )

    def call_start(d, carry):
        call_copy(d, box).start()
        return carry

    lax.fori_loop(1, BOXES, call_start, 0)

    rows = jnp.clip((sources[...] - (box * LB - LB)) * CP, 0, EMPTY - CP)
    rows = jnp.where(sources[...] >= 0, rows, EMPTY)
    index_v[...] = jnp.concatenate([rows, jnp.full((192 - SLOTS, LB), EMPTY, I32)], 0)
    index_copy = pltpu.make_async_copy(index_v, index_s, index_sem)
    index_copy.start()

    load_a.wait()
    for half in range(2):
        byrow[:, (half * KP + K) * 8 : (half + 1) * KP * 8, :] = jnp.zeros((24, (KP - K) * 8, 128), F32)
    eye = jnp.where(
        lax.broadcasted_iota(I32, (192, SLOTS), 0) == lax.broadcasted_iota(I32, (192, SLOTS), 1), 1.0, 0.0
    ).astype(BF16)

    def turn_slots(i, carry):
        gap = jnp.zeros((128, SLOTS), BF16)
        for r in range(7):
            q = i * 7 + r
            block = below(transfer_v[q].astype(F32), KP).astype(BF16)
            both = dot_nt(eye, jnp.concatenate([block, gap, block], 0))
            byrow[:, pl.ds(pl.multiple_of(q * 8, 8), 8), :] = both[:, :128].reshape(24, 8, 128)
            byrow[:, pl.ds(pl.multiple_of((KP + q) * 8, 8), 8), :] = both[:, 128:].reshape(24, 8, 128)
        return carry

    lax.fori_loop(0, 7, turn_slots, 0)

    def pack_slots(g, carry):
        for r in range(8):
            weights[g * 8 + r] = byrow[g, pl.ds(r, 128, stride=8), :].astype(BF16)
        return carry

    lax.fori_loop(0, 24, pack_slots, 0)

    load_b.wait()
    class_row = jnp.concatenate([cclass[0:1, :], cclass[1:2, :]], 1)
    class_hot = onehot_rows(class_row, CLASSES)

    def pick_classes(i, carry):
        blocks = [below(ctransfer_v[i * 7 + r].astype(F32), 56).astype(BF16) for r in range(7)]
        picked32[pl.ds(pl.multiple_of(i * 392, 8), 392), :] = jnp.dot(
            jnp.concatenate(blocks, 0), class_hot, preferred_element_type=F32
        )
        return carry

    lax.fori_loop(0, 7, pick_classes, 0)
    index_copy.wait()

    table[1024:2048, :] = own32[...]
    table[3072:3080, :] = jnp.zeros((8, 128), F32)
    for copy in halos:
        copy.wait()
    table[0:1024, :] = before[...].astype(F32)
    table[2048:3072, :] = after[...].astype(F32)

    def block(width, slots, tb):
        def chunk(jc, acc):
            def pick(jj, t):
                start = index_s.at[pl.ds(jj, 193 - slots), pl.ds(t, LB + 1 - width)]
                return table[pl.ds(start[jc * slots, tb * width], 8), :]

            parts = []
            for jj in range(slots):
                pairs = [
                    jnp.concatenate([pick(jj, t), pick(jj, t + 1)], 0).astype(BF16) for t in range(0, width, 2)
                ]
                parts.append(jnp.concatenate(pairs, 0))
            lhs = jnp.concatenate(parts, 1)
            rhs = jnp.concatenate([weights[jc * slots + jj] for jj in range(slots)], 1)
            return acc + dot_nt(lhs, rhs)

        total = lax.fori_loop(0, 192 // slots, chunk, jnp.zeros((width * CP, 128), F32))
        far32[pl.ds(pl.multiple_of(tb * width * CP, width * CP), width * CP), :] = total

    def chan_copy(tb, d, sender):
        part = local.at[sender, pl.ds(pl.multiple_of(tb * 32, 32), 32)]
        return pltpu.make_async_remote_copy(
            src_ref=part, dst_ref=part, send_sem=chan_send.at[tb, d], recv_sem=chan_recv.at[tb, sender],
            device_id={"chan": lax.rem(chan + d, CHANS)}, device_id_type=MESH,
        )

    def finish(tb, carry):
        rows = pl.ds(pl.multiple_of(tb * 256, 256), 256)
        far32[rows, :] += local32[rows, :]
        for pair in range(CP):
            part = far32[pl.ds(tb * 256 + pair, 32, stride=CP), :]
            local[chan, pl.ds(pl.multiple_of(tb * 32, 32), 32), pair * 128 : pair * 128 + 128] = part.astype(BF16)
        for d in (3, 1, 2):
            chan_copy(tb, d, chan).start()
        return carry

    block(64, 32, 0)

    def call_wait(d, carry):
        call_copy(d, box).wait_send()
        call_copy(d, lax.rem(box + BOXES - d, BOXES)).wait_recv()
        return carry

    lax.fori_loop(1, BOXES, call_wait, 0)
    source_row = jnp.concatenate([csource[0:1, :], csource[1:2, :]], 1)
    source_hot = onehot_rows(source_row, 128)
    own32[...] = call[...].astype(F32)
    for pair in range(CP):
        flat = own32[pl.ds(pair, 128, stride=CP), :].T.astype(BF16)
        source32[pair * 128 : pair * 128 + 128, :] = jnp.dot(flat, source_hot, preferred_element_type=F32)
    first_half = lax.broadcasted_iota(I32, (16, 128), 1) < KP

    def contract(i, acc):
        lhs, rhs = [], []
        for r in range(7):
            k = i * 7 + r
            rhs.append(picked32[pl.ds(k, K, stride=56), :].astype(BF16))
            both = jnp.concatenate(
                [source32[pl.ds(k, 8, stride=128), :], source32[pl.ds(KP + k, 8, stride=128), :]], 0
            )
            lhs.append(
                jnp.concatenate([jnp.where(first_half, both, 0.0), jnp.where(first_half, 0.0, both)], 0).astype(BF16)
            )
        return acc + dot_nt(jnp.concatenate(lhs, 1), jnp.concatenate(rhs, 1))

    both = lax.fori_loop(0, 7, contract, jnp.zeros((32, K), F32))
    both = jnp.concatenate([both, jnp.zeros((32, 128 - K), F32)], 1)
    coarse_local = jnp.concatenate(
        [both[0:8] + pltpu.roll(both[8:16], KP, 1), both[16:24] + pltpu.roll(both[24:32], KP, 1)], 0
    ).astype(BF16)
    tables = octant_tables(down, wide)
    for o in range(8):
        mid = dot_nt(coarse_local, tables[o])
        mid32[o * 8 : o * 8 + 8, :] = mid[:8]
        mid32[64 + o * 8 : 64 + o * 8 + 8, :] = mid[8:]
    mids = mid32[...].astype(BF16)
    for o in range(8):
        part = dot_nt(mids, tables[o])
        for m in range(16):
            local32[m * 64 + o * 8 : m * 64 + o * 8 + 8, :] = part[m * 8 : m * 8 + 8]

    lax.fori_loop(0, 2, finish, 0)

    def block_and_finish(tb, carry):
        block(32, 64, tb)
        finish(tb, 0)
        return carry

    lax.fori_loop(2, 4, block_and_finish, 0)

    mine = pl.ds(pl.multiple_of(chan * CH, CH), CH)
    mixes = jnp.concatenate([mix[l, mine, :] for l in range(DEG)], 0)
    lane = lax.broadcasted_iota(I32, (CH, 512), 1) % KP
    ahead = lax.broadcasted_iota(I32, (64, 512), 0) - lax.broadcasted_iota(I32, (64, 512), 1) // KP
    mixed = acc.at[0 : K * CH]
    mixed[...] = jnp.zeros((K * CH, LB), F32)
    for d in (0, 3, 1, 2):
        sender = lax.rem(chan + CHANS - d, CHANS)
        if d:
            for tb in range(4):
                chan_copy(tb, d, sender).wait_recv()

        def blend(i, carry):
            spread = jnp.where(ahead == sender * CH + i * 8, 1.0, 0.0).astype(BF16)
            weight = jnp.dot(mixes, spread, preferred_element_type=F32)
            lhs = jnp.concatenate(
                [
                    jnp.where(lane == k, weight[CH * DEGREE[k] : CH * DEGREE[k] + CH], 0.0).astype(BF16)
                    for k in range(K)
                ],
                0,
            )
            mixed[...] += dot_nt(lhs, local[sender, :, pl.ds(pl.multiple_of(i * 512, 512), 512)])
            return carry

        lax.fori_loop(0, 2, blend, 0)
    out[...] = mixed[...].astype(BF16)

    def chan_wait(tb, carry):
        for d in range(1, CHANS):
            chan_copy(tb, d, chan).wait_send()
        return carry

    lax.fori_loop(0, 4, chan_wait, 0)


def field_kernel(harm, leaf, mixed, out):
    step = 1024

    def turn(i, carry):
        at = pl.ds(pl.multiple_of(i * step, step), step)
        picked = jnp.dot(mixed[...], onehot_rows(leaf[:, at], LB), preferred_element_type=F32)
        h = harm[:, at].astype(F32)
        total = jnp.zeros((CH, step), F32)
        for k in range(K):
            total += h[k : k + 1] * picked[k * CH : k * CH + CH]
        out[:, at] = total.astype(BF16)
        return carry

    lax.fori_loop(0, ATOMS // step, turn, 0)


def on_device(
    features, harmonics, atom_leaf, leaf_sources, coarse_sources, coarse_class,
    child_to_parent, parent_to_child, leaf_transfer, coarse_transfer, mix_weight,
):
    params = dict(vmem_limit_bytes=60 << 20)
    leaf_row = atom_leaf.reshape(1, ATOMS)
    mixed = pl.pallas_call(
        far_kernel,
        out_shape=jax.ShapeDtypeStruct((K * CH, LB), BF16),
        in_specs=[VMEM] * 9 + [ANY] * 2,
        out_specs=VMEM,
        scratch_shapes=[
            pltpu.VMEM((CHANS, LB, 1024), BF16),
            pltpu.VMEM((KP * CH, LB), F32),
            pltpu.VMEM((1024, 128), F32),
            pltpu.VMEM((1024, 128), BF16),
            pltpu.VMEM((1024, 128), BF16),
            pltpu.VMEM((1024, 128), BF16),
            pltpu.VMEM((128, 128), F32),
            pltpu.VMEM((KP * 8, 128), F32),
            pltpu.VMEM((BOXES * 16, 128), BF16),
            pltpu.VMEM((K, K, SLOTS), BF16),
            pltpu.VMEM((K, K, CLASSES), BF16),
            pltpu.VMEM((24, 1024, 128), F32),
            pltpu.VMEM((192, 128, 128), BF16),
            pltpu.VMEM((192, LB), I32),
            pltpu.SMEM((192, LB), I32),
            pltpu.VMEM((EMPTY + 8, 128), F32),
            pltpu.VMEM((1024, 128), F32),
            pltpu.VMEM((1024, 128), F32),
            pltpu.VMEM((K * 56, 128), F32),
            pltpu.VMEM((1024, 128), F32),
            pltpu.SemaphoreType.DMA((2,)),
            pltpu.SemaphoreType.DMA,
            pltpu.SemaphoreType.DMA((2,)),
            pltpu.SemaphoreType.DMA((2,)),
            pltpu.SemaphoreType.DMA((BOXES,)),
            pltpu.SemaphoreType.DMA((BOXES,)),
            pltpu.SemaphoreType.DMA((4, CHANS)),
            pltpu.SemaphoreType.DMA((4, CHANS)),
        ],
        compiler_params=pltpu.CompilerParams(collective_id=0, has_side_effects=True, **params),
        name="far",
    )(
        features, harmonics, leaf_row, leaf_sources.T, coarse_sources, coarse_class,
        child_to_parent.transpose(1, 0, 2), parent_to_child.transpose(1, 0, 2), mix_weight,
        leaf_transfer.transpose(1, 2, 0), coarse_transfer.transpose(1, 2, 0),
    )

    return pl.pallas_call(
        field_kernel,
        out_shape=jax.ShapeDtypeStruct((CH, ATOMS), BF16),
        in_specs=[VMEM] * 3,
        out_specs=VMEM,
        compiler_params=pltpu.CompilerParams(**params),
        name="field",
    )(harmonics, leaf_row, mixed)


def solution(mesh):
    placed = (
        P("chan", "box"), P(None, "box"), P("box"), P("box", None), P("box", None), P("box", None),
        P(), P(), P(), P(), P(),
    )
    return jax.shard_map(
        on_device, mesh=mesh, in_specs=placed, out_specs=P("chan", "box"), check_vma=False
    )
```

```python
import jax
import jax.numpy as jnp
import numpy as np
from jax import lax
from jax.experimental import pallas as pl
from jax.experimental.pallas import tpu as pltpu
from jax.sharding import PartitionSpec as P

F32 = jnp.float32
BF16 = jnp.bfloat16
I32 = jnp.int32
MESH = pl.DeviceIdType.MESH
K = 49
KP = 64
CH = 16
CP = 8
LB = 128
ATOMS = 8192
SLOTS = 189
CLASSES = 316
BOXES = 64
GROUP = 16
PLANES = 4
CHANS = 4
EMPTY = 3 * LB * CP
NT = (((1,), (1,)), ((), ()))
VMEM = pl.BlockSpec(memory_space=pltpu.VMEM)
ANY = pl.BlockSpec(memory_space=pl.ANY)
DEG = 7
DEGREE = [int(np.sqrt(k)) for k in range(K)]


def dot_nt(a, b):
    return lax.dot_general(a, b, NT, preferred_element_type=F32)


def below(block, rows):
    return jnp.concatenate([block, jnp.zeros((rows - block.shape[0], block.shape[1]), block.dtype)], 0)


def octant_tables(ref, wide):
    wide[...] = jnp.zeros_like(wide)
    wide[0 : K * 8, 0:K] = ref[...].astype(F32).reshape(K * 8, K)
    tables = []
    for o in range(8):
        part = wide[pl.ds(o, KP, stride=8), :]
        tables.append(jnp.concatenate([part, pltpu.roll(part, KP, 1)], 0).astype(BF16))
    return tables


def onehot_rows(row, count):
    shape = (count, row.shape[1])
    return jnp.where(row == lax.broadcasted_iota(I32, shape, 0), 1.0, 0.0).astype(BF16)


def far_kernel(
    feat, harm, leaf, sources, csource, cclass, up, down, mix, transfer, ctransfer,
    out,
    local, acc, own32, own, before, after, mid32, wide, call, transfer_v, ctransfer_v, byrow, weights,
    index_v, index_s, table, far32, local32, picked32, source32,
    load_sem, index_sem, halo_send, halo_recv, call_send, call_recv, plane_send, plane_recv, chan_send, chan_recv,
):
    box = lax.axis_index("box")
    chan = lax.axis_index("chan")
    load_a = pltpu.make_async_copy(transfer, transfer_v, load_sem.at[0])
    load_b = pltpu.make_async_copy(ctransfer, ctransfer_v, load_sem.at[1])
    load_a.start()
    load_b.start()
    barrier = pltpu.get_barrier_semaphore()

    ring = lax.rem(box, GROUP)
    plane = box - ring

    def beside(d):
        return {"box": plane + lax.rem(ring + d, GROUP)}

    def across(e):
        return {"box": lax.rem(box + e * GROUP, BOXES)}

    right = {"box": lax.rem(box + 1, BOXES)}
    left = {"box": lax.rem(box + BOXES - 1, BOXES)}

    def greet(d, carry):
        pl.semaphore_signal(barrier, inc=1, device_id=beside(d), device_id_type=MESH)
        return carry

    lax.fori_loop(1, GROUP, greet, 0)
    others = [right, left] + [across(e) for e in range(1, PLANES)]
    others += [{"chan": lax.rem(chan + d, CHANS)} for d in range(1, CHANS)]
    for where in others:
        pl.semaphore_signal(barrier, inc=1, device_id=where, device_id_type=MESH)

    step = 1024
    acc[...] = jnp.zeros_like(acc)

    def turn(i, carry):
        at = pl.ds(pl.multiple_of(i * step, step), step)
        h = harm[:, at]
        f = feat[:, at]
        products = jnp.concatenate([h[k : k + 1] * f for k in range(K)], 0)
        acc[0 : K * CH, :] += dot_nt(products, onehot_rows(leaf[:, at], LB))
        return carry

    lax.fori_loop(0, ATOMS // step, turn, 0)
    for pair in range(CP):
        both = jnp.concatenate([acc[pl.ds(2 * pair + p, KP, stride=CH), :] for p in range(2)], 0)
        own32[pl.ds(pair, LB, stride=CP), :] = both.T.astype(BF16).astype(F32)
    own[...] = own32[...].astype(BF16)

    pl.semaphore_wait(barrier, GROUP - 1 + len(others))
    halos = [
        pltpu.make_async_remote_copy(
            src_ref=own, dst_ref=slot, send_sem=halo_send.at[i], recv_sem=halo_recv.at[i],
            device_id=where, device_id_type=MESH,
        )
        for i, (slot, where) in enumerate(((before, right), (after, left)))
    ]
    for copy in halos:
        copy.start()

    tables = octant_tables(up, wide)
    children = own32[...].reshape(16, 8, CP, 128)
    mid = jnp.zeros((128, 128), F32)
    for o in range(8):
        mid += dot_nt(children[:, o].reshape(128, 128).astype(BF16), tables[o])
    mid32[...] = mid.astype(BF16).astype(F32)
    mids = mid32[...].reshape(2, 8, CP, 128)
    coarse = jnp.zeros((16, 128), F32)
    for o in range(8):
        coarse += dot_nt(mids[:, o].reshape(16, 128).astype(BF16), tables[o])
    mine = call.at[pl.ds(pl.multiple_of(box * 16, 16), 16)]
    mine[...] = coarse.astype(BF16)

    def call_copy(d, sender):
        rows = call.at[pl.ds(pl.multiple_of((plane + sender) * 16, 16), 16)]
        return pltpu.make_async_remote_copy(
            src_ref=rows, dst_ref=rows, send_sem=call_send.at[d], recv_sem=call_recv.at[sender],
            device_id=beside(d), device_id_type=MESH,
        )

    def plane_copy(e, sender):
        rows = call.at[pl.ds(pl.multiple_of(sender * 16, 256), 256)]
        slot = lax.div(sender, GROUP)
        return pltpu.make_async_remote_copy(
            src_ref=rows, dst_ref=rows, send_sem=plane_send.at[e], recv_sem=plane_recv.at[slot],
            device_id=across(e), device_id_type=MESH,
        )

    def call_start(d, carry):
        call_copy(d, ring).start()
        return carry

    lax.fori_loop(1, GROUP, call_start, 0)

    rows = jnp.clip((sources[...] - (box * LB - LB)) * CP, 0, EMPTY - CP)
    rows = jnp.where(sources[...] >= 0, rows, EMPTY)
    index_v[...] = jnp.concatenate([rows, jnp.full((192 - SLOTS, LB), EMPTY, I32)], 0)
    index_copy = pltpu.make_async_copy(index_v, index_s, index_sem)
    index_copy.start()

    load_a.wait()
    for half in range(2):
        byrow[:, (half * KP + K) * 8 : (half + 1) * KP * 8, :] = jnp.zeros((24, (KP - K) * 8, 128), F32)
    eye = jnp.where(
        lax.broadcasted_iota(I32, (192, SLOTS), 0) == lax.broadcasted_iota(I32, (192, SLOTS), 1), 1.0, 0.0
    ).astype(BF16)

    def turn_slots(i, carry):
        gap = jnp.zeros((128, SLOTS), BF16)
        for r in range(7):
            q = i * 7 + r
            block = below(transfer_v[q].astype(F32), KP).astype(BF16)
            both = dot_nt(eye, jnp.concatenate([block, gap, block], 0))
            byrow[:, pl.ds(pl.multiple_of(q * 8, 8), 8), :] = both[:, :128].reshape(24, 8, 128)
            byrow[:, pl.ds(pl.multiple_of((KP + q) * 8, 8), 8), :] = both[:, 128:].reshape(24, 8, 128)
        return carry

    lax.fori_loop(0, 7, turn_slots, 0)

    def pack_slots(g, carry):
        for r in range(8):
            weights[g * 8 + r] = byrow[g, pl.ds(r, 128, stride=8), :].astype(BF16)
        return carry

    lax.fori_loop(0, 24, pack_slots, 0)

    load_b.wait()
    class_row = jnp.concatenate([cclass[0:1, :], cclass[1:2, :]], 1)
    class_hot = onehot_rows(class_row, CLASSES)

    def pick_classes(i, carry):
        blocks = [below(ctransfer_v[i * 7 + r].astype(F32), 56).astype(BF16) for r in range(7)]
        picked32[pl.ds(pl.multiple_of(i * 392, 8), 392), :] = jnp.dot(
            jnp.concatenate(blocks, 0), class_hot, preferred_element_type=F32
        )
        return carry

    lax.fori_loop(0, 7, pick_classes, 0)
    index_copy.wait()

    table[1024:2048, :] = own32[...]
    table[3072:3080, :] = jnp.zeros((8, 128), F32)

    def call_wait(d, carry):
        call_copy(d, ring).wait_send()
        call_copy(d, lax.rem(ring + GROUP - d, GROUP)).wait_recv()
        return carry

    lax.fori_loop(1, GROUP, call_wait, 0)
    for e in range(1, PLANES):
        plane_copy(e, plane).start()
    for copy in halos:
        copy.wait()
    table[0:1024, :] = before[...].astype(F32)
    table[2048:3072, :] = after[...].astype(F32)

    def block(width, slots, tb):
        def chunk(jc, acc):
            def pick(jj, t):
                start = index_s.at[pl.ds(jj, 193 - slots), pl.ds(t, LB + 1 - width)]
                return table[pl.ds(start[jc * slots, tb * width], 8), :]

            parts = []
            for jj in range(slots):
                pairs = [
                    jnp.concatenate([pick(jj, t), pick(jj, t + 1)], 0).astype(BF16) for t in range(0, width, 2)
                ]
                parts.append(jnp.concatenate(pairs, 0))
            lhs = jnp.concatenate(parts, 1)
            rhs = jnp.concatenate([weights[jc * slots + jj] for jj in range(slots)], 1)
            return acc + dot_nt(lhs, rhs)

        total = lax.fori_loop(0, 192 // slots, chunk, jnp.zeros((width * CP, 128), F32))
        far32[pl.ds(pl.multiple_of(tb * width * CP, width * CP), width * CP), :] = total

    def chan_copy(tb, d, sender):
        part = local.at[sender, pl.ds(pl.multiple_of(tb * 32, 32), 32)]
        return pltpu.make_async_remote_copy(
            src_ref=part, dst_ref=part, send_sem=chan_send.at[tb, d], recv_sem=chan_recv.at[tb, sender],
            device_id={"chan": lax.rem(chan + d, CHANS)}, device_id_type=MESH,
        )

    def finish(tb, carry):
        rows = pl.ds(pl.multiple_of(tb * 256, 256), 256)
        far32[rows, :] += local32[rows, :]
        for pair in range(CP):
            part = far32[pl.ds(tb * 256 + pair, 32, stride=CP), :]
            local[chan, pl.ds(pl.multiple_of(tb * 32, 32), 32), pair * 128 : pair * 128 + 128] = part.astype(BF16)
        for d in (3, 1, 2):
            chan_copy(tb, d, chan).start()
        return carry

    block(64, 32, 0)

    for e in range(1, PLANES):
        plane_copy(e, plane).wait_send()
        plane_copy(e, lax.rem(plane + BOXES - e * GROUP, BOXES)).wait_recv()
    source_row = jnp.concatenate([csource[0:1, :], csource[1:2, :]], 1)
    source_hot = onehot_rows(source_row, 128)
    own32[...] = call[...].astype(F32)
    for pair in range(CP):
        flat = own32[pl.ds(pair, 128, stride=CP), :].T.astype(BF16)
        source32[pair * 128 : pair * 128 + 128, :] = jnp.dot(flat, source_hot, preferred_element_type=F32)
    first_half = lax.broadcasted_iota(I32, (16, 128), 1) < KP

    def contract(i, acc):
        lhs, rhs = [], []
        for r in range(7):
            k = i * 7 + r
            rhs.append(picked32[pl.ds(k, K, stride=56), :].astype(BF16))
            both = jnp.concatenate(
                [source32[pl.ds(k, 8, stride=128), :], source32[pl.ds(KP + k, 8, stride=128), :]], 0
            )
            lhs.append(
                jnp.concatenate([jnp.where(first_half, both, 0.0), jnp.where(first_half, 0.0, both)], 0).astype(BF16)
            )
        return acc + dot_nt(jnp.concatenate(lhs, 1), jnp.concatenate(rhs, 1))

    both = lax.fori_loop(0, 7, contract, jnp.zeros((32, K), F32))
    both = jnp.concatenate([both, jnp.zeros((32, 128 - K), F32)], 1)
    coarse_local = jnp.concatenate(
        [both[0:8] + pltpu.roll(both[8:16], KP, 1), both[16:24] + pltpu.roll(both[24:32], KP, 1)], 0
    ).astype(BF16)
    tables = octant_tables(down, wide)
    for o in range(8):
        mid = dot_nt(coarse_local, tables[o])
        mid32[o * 8 : o * 8 + 8, :] = mid[:8]
        mid32[64 + o * 8 : 64 + o * 8 + 8, :] = mid[8:]
    mids = mid32[...].astype(BF16)
    for o in range(8):
        part = dot_nt(mids, tables[o])
        for m in range(16):
            local32[m * 64 + o * 8 : m * 64 + o * 8 + 8, :] = part[m * 8 : m * 8 + 8]

    lax.fori_loop(0, 2, finish, 0)

    def block_and_finish(tb, carry):
        block(32, 64, tb)
        finish(tb, 0)
        return carry

    lax.fori_loop(2, 4, block_and_finish, 0)

    mine = pl.ds(pl.multiple_of(chan * CH, CH), CH)
    mixes = jnp.concatenate([mix[l, mine, :] for l in range(DEG)], 0)
    lane = lax.broadcasted_iota(I32, (CH, 512), 1) % KP
    ahead = lax.broadcasted_iota(I32, (64, 512), 0) - lax.broadcasted_iota(I32, (64, 512), 1) // KP
    mixed = acc.at[0 : K * CH]
    mixed[...] = jnp.zeros((K * CH, LB), F32)
    for d in (0, 3, 1, 2):
        sender = lax.rem(chan + CHANS - d, CHANS)
        if d:
            for tb in range(4):
                chan_copy(tb, d, sender).wait_recv()

        def blend(i, carry):
            spread = jnp.where(ahead == sender * CH + i * 8, 1.0, 0.0).astype(BF16)
            weight = jnp.dot(mixes, spread, preferred_element_type=F32)
            lhs = jnp.concatenate(
                [
                    jnp.where(lane == k, weight[CH * DEGREE[k] : CH * DEGREE[k] + CH], 0.0).astype(BF16)
                    for k in range(K)
                ],
                0,
            )
            mixed[...] += dot_nt(lhs, local[sender, :, pl.ds(pl.multiple_of(i * 512, 512), 512)])
            return carry

        lax.fori_loop(0, 2, blend, 0)
    out[...] = mixed[...].astype(BF16)

    def chan_wait(tb, carry):
        for d in range(1, CHANS):
            chan_copy(tb, d, chan).wait_send()
        return carry

    lax.fori_loop(0, 4, chan_wait, 0)


def field_kernel(harm, leaf, mixed, out):
    step = 1024

    def turn(i, carry):
        at = pl.ds(pl.multiple_of(i * step, step), step)
        picked = jnp.dot(mixed[...], onehot_rows(leaf[:, at], LB), preferred_element_type=F32)
        h = harm[:, at].astype(F32)
        total = jnp.zeros((CH, step), F32)
        for k in range(K):
            total += h[k : k + 1] * picked[k * CH : k * CH + CH]
        out[:, at] = total.astype(BF16)
        return carry

    lax.fori_loop(0, ATOMS // step, turn, 0)


def on_device(
    features, harmonics, atom_leaf, leaf_sources, coarse_sources, coarse_class,
    child_to_parent, parent_to_child, leaf_transfer, coarse_transfer, mix_weight,
):
    params = dict(vmem_limit_bytes=60 << 20)
    leaf_row = atom_leaf.reshape(1, ATOMS)
    mixed = pl.pallas_call(
        far_kernel,
        out_shape=jax.ShapeDtypeStruct((K * CH, LB), BF16),
        in_specs=[VMEM] * 9 + [ANY] * 2,
        out_specs=VMEM,
        scratch_shapes=[
            pltpu.VMEM((CHANS, LB, 1024), BF16),
            pltpu.VMEM((KP * CH, LB), F32),
            pltpu.VMEM((1024, 128), F32),
            pltpu.VMEM((1024, 128), BF16),
            pltpu.VMEM((1024, 128), BF16),
            pltpu.VMEM((1024, 128), BF16),
            pltpu.VMEM((128, 128), F32),
            pltpu.VMEM((KP * 8, 128), F32),
            pltpu.VMEM((BOXES * 16, 128), BF16),
            pltpu.VMEM((K, K, SLOTS), BF16),
            pltpu.VMEM((K, K, CLASSES), BF16),
            pltpu.VMEM((24, 1024, 128), F32),
            pltpu.VMEM((192, 128, 128), BF16),
            pltpu.VMEM((192, LB), I32),
            pltpu.SMEM((192, LB), I32),
            pltpu.VMEM((EMPTY + 8, 128), F32),
            pltpu.VMEM((1024, 128), F32),
            pltpu.VMEM((1024, 128), F32),
            pltpu.VMEM((K * 56, 128), F32),
            pltpu.VMEM((1024, 128), F32),
            pltpu.SemaphoreType.DMA((2,)),
            pltpu.SemaphoreType.DMA,
            pltpu.SemaphoreType.DMA((2,)),
            pltpu.SemaphoreType.DMA((2,)),
            pltpu.SemaphoreType.DMA((GROUP,)),
            pltpu.SemaphoreType.DMA((GROUP,)),
            pltpu.SemaphoreType.DMA((PLANES,)),
            pltpu.SemaphoreType.DMA((PLANES,)),
            pltpu.SemaphoreType.DMA((4, CHANS)),
            pltpu.SemaphoreType.DMA((4, CHANS)),
        ],
        compiler_params=pltpu.CompilerParams(collective_id=0, has_side_effects=True, **params),
        name="far",
    )(
        features, harmonics, leaf_row, leaf_sources.T, coarse_sources, coarse_class,
        child_to_parent.transpose(1, 0, 2), parent_to_child.transpose(1, 0, 2), mix_weight,
        leaf_transfer.transpose(1, 2, 0), coarse_transfer.transpose(1, 2, 0),
    )

    return pl.pallas_call(
        field_kernel,
        out_shape=jax.ShapeDtypeStruct((CH, ATOMS), BF16),
        in_specs=[VMEM] * 3,
        out_specs=VMEM,
        compiler_params=pltpu.CompilerParams(**params),
        name="field",
    )(harmonics, leaf_row, mixed)


def solution(mesh):
    placed = (
        P("chan", "box"), P(None, "box"), P("box"), P("box", None), P("box", None), P("box", None),
        P(), P(), P(), P(), P(),
    )
    return jax.shard_map(
        on_device, mesh=mesh, in_specs=placed, out_specs=P("chan", "box"), check_vma=False
    )
```

```python
import jax
import jax.numpy as jnp
import numpy as np
from jax import lax
from jax.experimental import pallas as pl
from jax.experimental.pallas import tpu as pltpu
from jax.sharding import PartitionSpec as P

F32 = jnp.float32
BF16 = jnp.bfloat16
I32 = jnp.int32
MESH = pl.DeviceIdType.MESH
K = 49
KP = 64
CH = 16
CP = 8
LB = 128
ATOMS = 8192
SLOTS = 189
CLASSES = 316
BOXES = 64
GROUP = 16
PLANES = 4
CHANS = 4
EMPTY = 3 * LB * CP
NT = (((1,), (1,)), ((), ()))
VMEM = pl.BlockSpec(memory_space=pltpu.VMEM)
ANY = pl.BlockSpec(memory_space=pl.ANY)
DEG = 7
DEGREE = [int(np.sqrt(k)) for k in range(K)]


def dot_nt(a, b):
    return lax.dot_general(a, b, NT, preferred_element_type=F32)


def below(block, rows):
    return jnp.concatenate([block, jnp.zeros((rows - block.shape[0], block.shape[1]), block.dtype)], 0)


def octant_tables(ref, wide):
    wide[...] = jnp.zeros_like(wide)
    wide[0 : K * 8, 0:K] = ref[...].astype(F32).reshape(K * 8, K)
    tables = []
    for o in range(8):
        part = wide[pl.ds(o, KP, stride=8), :]
        tables.append(jnp.concatenate([part, pltpu.roll(part, KP, 1)], 0).astype(BF16))
    return tables


def onehot_rows(row, count):
    shape = (count, row.shape[1])
    return jnp.where(row == lax.broadcasted_iota(I32, shape, 0), 1.0, 0.0).astype(BF16)


def far_kernel(
    feat, harm, leaf, sources, csource, cclass, up, down, mix, transfer, ctransfer,
    out,
    local, mixed16, acc, own32, own, before, after, mid32, wide, call, transfer_v, ctransfer_v, byrow, weights,
    index_v, index_s, table, far32, local32, picked32, source32,
    load_sem, index_sem, halo_send, halo_recv, call_send, call_recv, plane_send, plane_recv, chan_send, chan_recv,
):
    box = lax.axis_index("box")
    chan = lax.axis_index("chan")
    load_a = pltpu.make_async_copy(transfer, transfer_v, load_sem.at[0])
    load_b = pltpu.make_async_copy(ctransfer, ctransfer_v, load_sem.at[1])
    load_a.start()
    load_b.start()
    barrier = pltpu.get_barrier_semaphore()

    ring = lax.rem(box, GROUP)
    plane = box - ring

    def beside(d):
        return {"box": plane + lax.rem(ring + d, GROUP)}

    def across(e):
        return {"box": lax.rem(box + e * GROUP, BOXES)}

    right = {"box": lax.rem(box + 1, BOXES)}
    left = {"box": lax.rem(box + BOXES - 1, BOXES)}

    def greet(d, carry):
        pl.semaphore_signal(barrier, inc=1, device_id=beside(d), device_id_type=MESH)
        return carry

    lax.fori_loop(1, GROUP, greet, 0)
    others = [right, left] + [across(e) for e in range(1, PLANES)]
    others += [{"chan": lax.rem(chan + d, CHANS)} for d in range(1, CHANS)]
    for where in others:
        pl.semaphore_signal(barrier, inc=1, device_id=where, device_id_type=MESH)

    step = 1024
    acc[...] = jnp.zeros_like(acc)

    def turn(i, carry):
        at = pl.ds(pl.multiple_of(i * step, step), step)
        h = harm[:, at]
        f = feat[:, at]
        products = jnp.concatenate([h[k : k + 1] * f for k in range(K)], 0)
        acc[0 : K * CH, :] += dot_nt(products, onehot_rows(leaf[:, at], LB))
        return carry

    lax.fori_loop(0, ATOMS // step, turn, 0)
    for pair in range(CP):
        both = jnp.concatenate([acc[pl.ds(2 * pair + p, KP, stride=CH), :] for p in range(2)], 0)
        own32[pl.ds(pair, LB, stride=CP), :] = both.T.astype(BF16).astype(F32)
    own[...] = own32[...].astype(BF16)

    pl.semaphore_wait(barrier, GROUP - 1 + len(others))
    halos = [
        pltpu.make_async_remote_copy(
            src_ref=own, dst_ref=slot, send_sem=halo_send.at[i], recv_sem=halo_recv.at[i],
            device_id=where, device_id_type=MESH,
        )
        for i, (slot, where) in enumerate(((before, right), (after, left)))
    ]
    for copy in halos:
        copy.start()

    tables = octant_tables(up, wide)
    children = own32[...].reshape(16, 8, CP, 128)
    mid = jnp.zeros((128, 128), F32)
    for o in range(8):
        mid += dot_nt(children[:, o].reshape(128, 128).astype(BF16), tables[o])
    mid32[...] = mid.astype(BF16).astype(F32)
    mids = mid32[...].reshape(2, 8, CP, 128)
    coarse = jnp.zeros((16, 128), F32)
    for o in range(8):
        coarse += dot_nt(mids[:, o].reshape(16, 128).astype(BF16), tables[o])
    mine = call.at[pl.ds(pl.multiple_of(box * 16, 16), 16)]
    mine[...] = coarse.astype(BF16)

    def call_copy(d, sender):
        rows = call.at[pl.ds(pl.multiple_of((plane + sender) * 16, 16), 16)]
        return pltpu.make_async_remote_copy(
            src_ref=rows, dst_ref=rows, send_sem=call_send.at[d], recv_sem=call_recv.at[sender],
            device_id=beside(d), device_id_type=MESH,
        )

    def plane_copy(e, sender):
        rows = call.at[pl.ds(pl.multiple_of(sender * 16, 256), 256)]
        slot = lax.div(sender, GROUP)
        return pltpu.make_async_remote_copy(
            src_ref=rows, dst_ref=rows, send_sem=plane_send.at[e], recv_sem=plane_recv.at[slot],
            device_id=across(e), device_id_type=MESH,
        )

    def call_start(d, carry):
        call_copy(d, ring).start()
        return carry

    lax.fori_loop(1, GROUP, call_start, 0)

    rows = jnp.clip((sources[...] - (box * LB - LB)) * CP, 0, EMPTY - CP)
    rows = jnp.where(sources[...] >= 0, rows, EMPTY)
    index_v[...] = jnp.concatenate([rows, jnp.full((192 - SLOTS, LB), EMPTY, I32)], 0)
    index_copy = pltpu.make_async_copy(index_v, index_s, index_sem)
    index_copy.start()

    load_a.wait()
    for half in range(2):
        byrow[:, (half * KP + K) * 8 : (half + 1) * KP * 8, :] = jnp.zeros((24, (KP - K) * 8, 128), F32)
    eye = jnp.where(
        lax.broadcasted_iota(I32, (192, SLOTS), 0) == lax.broadcasted_iota(I32, (192, SLOTS), 1), 1.0, 0.0
    ).astype(BF16)

    def turn_slots(i, carry):
        gap = jnp.zeros((128, SLOTS), BF16)
        for r in range(7):
            q = i * 7 + r
            block = below(transfer_v[q].astype(F32), KP).astype(BF16)
            both = dot_nt(eye, jnp.concatenate([block, gap, block], 0))
            byrow[:, pl.ds(pl.multiple_of(q * 8, 8), 8), :] = both[:, :128].reshape(24, 8, 128)
            byrow[:, pl.ds(pl.multiple_of((KP + q) * 8, 8), 8), :] = both[:, 128:].reshape(24, 8, 128)
        return carry

    lax.fori_loop(0, 7, turn_slots, 0)

    def pack_slots(g, carry):
        for r in range(8):
            weights[g * 8 + r] = byrow[g, pl.ds(r, 128, stride=8), :].astype(BF16)
        return carry

    lax.fori_loop(0, 24, pack_slots, 0)

    load_b.wait()
    class_row = jnp.concatenate([cclass[0:1, :], cclass[1:2, :]], 1)
    class_hot = onehot_rows(class_row, CLASSES)

    def pick_classes(i, carry):
        blocks = [below(ctransfer_v[i * 7 + r].astype(F32), 56).astype(BF16) for r in range(7)]
        picked32[pl.ds(pl.multiple_of(i * 392, 8), 392), :] = jnp.dot(
            jnp.concatenate(blocks, 0), class_hot, preferred_element_type=F32
        )
        return carry

    lax.fori_loop(0, 7, pick_classes, 0)
    index_copy.wait()

    table[1024:2048, :] = own32[...]
    table[3072:3080, :] = jnp.zeros((8, 128), F32)

    def call_wait(d, carry):
        call_copy(d, ring).wait_send()
        call_copy(d, lax.rem(ring + GROUP - d, GROUP)).wait_recv()
        return carry

    lax.fori_loop(1, GROUP, call_wait, 0)
    for e in range(1, PLANES):
        plane_copy(e, plane).start()
    for copy in halos:
        copy.wait()
    table[0:1024, :] = before[...].astype(F32)
    table[2048:3072, :] = after[...].astype(F32)

    def block(width, slots, tb):
        def chunk(jc, acc):
            def pick(jj, t):
                start = index_s.at[pl.ds(jj, 193 - slots), pl.ds(t, LB + 1 - width)]
                return table[pl.ds(start[jc * slots, tb * width], 8), :]

            parts = []
            for jj in range(slots):
                pairs = [
                    jnp.concatenate([pick(jj, t), pick(jj, t + 1)], 0).astype(BF16) for t in range(0, width, 2)
                ]
                parts.append(jnp.concatenate(pairs, 0))
            lhs = jnp.concatenate(parts, 1)
            rhs = jnp.concatenate([weights[jc * slots + jj] for jj in range(slots)], 1)
            return acc + dot_nt(lhs, rhs)

        total = lax.fori_loop(0, 192 // slots, chunk, jnp.zeros((width * CP, 128), F32))
        far32[pl.ds(pl.multiple_of(tb * width * CP, width * CP), width * CP), :] = total

    def chan_copy(tb, d, sender):
        part = local.at[sender, pl.ds(pl.multiple_of(tb * 32, 32), 32)]
        return pltpu.make_async_remote_copy(
            src_ref=part, dst_ref=part, send_sem=chan_send.at[tb, d], recv_sem=chan_recv.at[tb, sender],
            device_id={"chan": lax.rem(chan + d, CHANS)}, device_id_type=MESH,
        )

    def finish(tb, carry):
        rows = pl.ds(pl.multiple_of(tb * 256, 256), 256)
        far32[rows, :] += local32[rows, :]
        for pair in range(CP):
            part = far32[pl.ds(tb * 256 + pair, 32, stride=CP), :]
            local[chan, pl.ds(pl.multiple_of(tb * 32, 32), 32), pair * 128 : pair * 128 + 128] = part.astype(BF16)
        for d in (3, 1, 2):
            chan_copy(tb, d, chan).start()
        return carry

    block(64, 32, 0)

    for e in range(1, PLANES):
        plane_copy(e, plane).wait_send()
        plane_copy(e, lax.rem(plane + BOXES - e * GROUP, BOXES)).wait_recv()
    source_row = jnp.concatenate([csource[0:1, :], csource[1:2, :]], 1)
    source_hot = onehot_rows(source_row, 128)
    own32[...] = call[...].astype(F32)
    for pair in range(CP):
        flat = own32[pl.ds(pair, 128, stride=CP), :].T.astype(BF16)
        source32[pair * 128 : pair * 128 + 128, :] = jnp.dot(flat, source_hot, preferred_element_type=F32)
    first_half = lax.broadcasted_iota(I32, (16, 128), 1) < KP

    def contract(i, acc):
        lhs, rhs = [], []
        for r in range(7):
            k = i * 7 + r
            rhs.append(picked32[pl.ds(k, K, stride=56), :].astype(BF16))
            both = jnp.concatenate(
                [source32[pl.ds(k, 8, stride=128), :], source32[pl.ds(KP + k, 8, stride=128), :]], 0
            )
            lhs.append(
                jnp.concatenate([jnp.where(first_half, both, 0.0), jnp.where(first_half, 0.0, both)], 0).astype(BF16)
            )
        return acc + dot_nt(jnp.concatenate(lhs, 1), jnp.concatenate(rhs, 1))

    both = lax.fori_loop(0, 7, contract, jnp.zeros((32, K), F32))
    both = jnp.concatenate([both, jnp.zeros((32, 128 - K), F32)], 1)
    coarse_local = jnp.concatenate(
        [both[0:8] + pltpu.roll(both[8:16], KP, 1), both[16:24] + pltpu.roll(both[24:32], KP, 1)], 0
    ).astype(BF16)
    tables = octant_tables(down, wide)
    for o in range(8):
        mid = dot_nt(coarse_local, tables[o])
        mid32[o * 8 : o * 8 + 8, :] = mid[:8]
        mid32[64 + o * 8 : 64 + o * 8 + 8, :] = mid[8:]
    mids = mid32[...].astype(BF16)
    for o in range(8):
        part = dot_nt(mids, tables[o])
        for m in range(16):
            local32[m * 64 + o * 8 : m * 64 + o * 8 + 8, :] = part[m * 8 : m * 8 + 8]

    lax.fori_loop(0, 2, finish, 0)

    def block_and_finish(tb, carry):
        block(32, 64, tb)
        finish(tb, 0)
        return carry

    lax.fori_loop(2, 4, block_and_finish, 0)

    mine = pl.ds(pl.multiple_of(chan * CH, CH), CH)
    mixes = jnp.concatenate([mix[l, mine, :] for l in range(DEG)], 0)
    lane = lax.broadcasted_iota(I32, (CH, 512), 1) % KP
    ahead = lax.broadcasted_iota(I32, (64, 512), 0) - lax.broadcasted_iota(I32, (64, 512), 1) // KP
    mixed = acc.at[0 : K * CH]
    mixed[...] = jnp.zeros((K * CH, LB), F32)
    for d in (0, 3, 1, 2):
        sender = lax.rem(chan + CHANS - d, CHANS)
        if d:
            for tb in range(4):
                chan_copy(tb, d, sender).wait_recv()

        def blend(i, carry):
            spread = jnp.where(ahead == sender * CH + i * 8, 1.0, 0.0).astype(BF16)
            weight = jnp.dot(mixes, spread, preferred_element_type=F32)
            lhs = jnp.concatenate(
                [
                    jnp.where(lane == k, weight[CH * DEGREE[k] : CH * DEGREE[k] + CH], 0.0).astype(BF16)
                    for k in range(K)
                ],
                0,
            )
            mixed[...] += dot_nt(lhs, local[sender, :, pl.ds(pl.multiple_of(i * 512, 512), 512)])
            return carry

        lax.fori_loop(0, 2, blend, 0)
    mixed16[...] = mixed[...].astype(BF16)

    def evaluate(i, carry):
        at = pl.ds(pl.multiple_of(i * step, step), step)
        picked = jnp.dot(mixed16[...], onehot_rows(leaf[:, at], LB), preferred_element_type=F32)
        h = harm[:, at].astype(F32)
        total = jnp.zeros((CH, step), F32)
        for k in range(K):
            total += h[k : k + 1] * picked[k * CH : k * CH + CH]
        out[:, at] = total.astype(BF16)
        return carry

    lax.fori_loop(0, ATOMS // step, evaluate, 0)

    def chan_wait(tb, carry):
        for d in range(1, CHANS):
            chan_copy(tb, d, chan).wait_send()
        return carry

    lax.fori_loop(0, 4, chan_wait, 0)


def on_device(
    features, harmonics, atom_leaf, leaf_sources, coarse_sources, coarse_class,
    child_to_parent, parent_to_child, leaf_transfer, coarse_transfer, mix_weight,
):
    params = dict(vmem_limit_bytes=60 << 20)
    leaf_row = atom_leaf.reshape(1, ATOMS)
    return pl.pallas_call(
        far_kernel,
        out_shape=jax.ShapeDtypeStruct((CH, ATOMS), BF16),
        in_specs=[VMEM] * 9 + [ANY] * 2,
        out_specs=VMEM,
        scratch_shapes=[
            pltpu.VMEM((CHANS, LB, 1024), BF16),
            pltpu.VMEM((K * CH, LB), BF16),
            pltpu.VMEM((KP * CH, LB), F32),
            pltpu.VMEM((1024, 128), F32),
            pltpu.VMEM((1024, 128), BF16),
            pltpu.VMEM((1024, 128), BF16),
            pltpu.VMEM((1024, 128), BF16),
            pltpu.VMEM((128, 128), F32),
            pltpu.VMEM((KP * 8, 128), F32),
            pltpu.VMEM((BOXES * 16, 128), BF16),
            pltpu.VMEM((K, K, SLOTS), BF16),
            pltpu.VMEM((K, K, CLASSES), BF16),
            pltpu.VMEM((24, 1024, 128), F32),
            pltpu.VMEM((192, 128, 128), BF16),
            pltpu.VMEM((192, LB), I32),
            pltpu.SMEM((192, LB), I32),
            pltpu.VMEM((EMPTY + 8, 128), F32),
            pltpu.VMEM((1024, 128), F32),
            pltpu.VMEM((1024, 128), F32),
            pltpu.VMEM((K * 56, 128), F32),
            pltpu.VMEM((1024, 128), F32),
            pltpu.SemaphoreType.DMA((2,)),
            pltpu.SemaphoreType.DMA,
            pltpu.SemaphoreType.DMA((2,)),
            pltpu.SemaphoreType.DMA((2,)),
            pltpu.SemaphoreType.DMA((GROUP,)),
            pltpu.SemaphoreType.DMA((GROUP,)),
            pltpu.SemaphoreType.DMA((PLANES,)),
            pltpu.SemaphoreType.DMA((PLANES,)),
            pltpu.SemaphoreType.DMA((4, CHANS)),
            pltpu.SemaphoreType.DMA((4, CHANS)),
        ],
        compiler_params=pltpu.CompilerParams(collective_id=0, has_side_effects=True, **params),
        name="far",
    )(
        features, harmonics, leaf_row, leaf_sources.T, coarse_sources, coarse_class,
        child_to_parent.transpose(1, 0, 2), parent_to_child.transpose(1, 0, 2), mix_weight,
        leaf_transfer.transpose(1, 2, 0), coarse_transfer.transpose(1, 2, 0),
    )


def solution(mesh):
    placed = (
        P("chan", "box"), P(None, "box"), P("box"), P("box", None), P("box", None), P("box", None),
        P(), P(), P(), P(), P(),
    )
    return jax.shard_map(
        on_device, mesh=mesh, in_specs=placed, out_specs=P("chan", "box"), check_vma=False
    )
```
